128 devices in a mesh: dp: 32 (over x, z, core), mp: 4 (over y).
Axes of the slice: x: 4, y: 4, z: 4, core: 2. Of those that a mesh axis runs over, the one named last changes fastest.
Arguments:
- hidden_in: bfloat16 [512, 8192], P(None, 'dp'), may hold values from -6 to 6
- gain_attn: float32 [8192], P('dp'), may hold values from 0.1 to 1.9
- w_query: bfloat16 [8192, 8192], P('dp', 'mp'), may hold values from -0.0625 to 0.0625
- w_keyval: bfloat16 [8192, 2, 1024], P('dp', None, 'mp'), may hold values from -0.0625 to 0.0625
- w_out: bfloat16 [8192, 8192], P(None, 'dp'), may hold values from -0.0625 to 0.0625
- key_cache: bfloat16 [512, 8, 192, 128], P('dp', 'mp'), may hold values from -210 to 210
- value_cache: bfloat16 [512, 8, 192, 128], P('dp', 'mp'), may hold values from -6 to 6
- lengths: int32 [512], P('dp'), may hold values from 2 to 192, as said below
- gain_final: float32 [8192], P('dp'), may hold values from 0.1 to 1.9
- w_vocab: bfloat16 [8192, 128256], P(None, ('dp', 'mp')), may hold values from -2.32019413 to 2.32019413
- pair_rows: int32 [512], replicated, may hold values from 0 to 511, each once
- grammar: int32 [256, 8064], P(None, ('dp', 'mp')), may hold values from 0 to 65535, as said below
Outputs:
- logprobs: float32 [256, 128256], P(None, ('dp', 'mp'))
The draws below stay inside these ranges and needn't reach their ends.
Inputs may be any that keep to these rules, and one draw needn't show every extreme that they name: `lengths`: every draw has a row of exactly 192 cached positions. `grammar`: bits past 1002 in a device's last word are ignored. `pair_rows`: each row appears exactly once.
All inputs are finite; a program needn't handle non-finite values.
Results may differ from the reference program's by a relative error of at most 0.0065.
Values may be sent and summed in bfloat16 or wider, within the bound.
No kernel may reach another device: no remote copies, remote signals or barrier semaphores. Data moves between devices by JAX's collectives and lax.ppermute only.
A program may use at most 128 MiB of HBM per device.

```python
import math
import jax
import jax.numpy as jnp
from jax import lax

D = 8192
H = 64
KVH = 8
HD = 128
V_DEV = 1002
LMAX = 192
WORDS = 63
VOCAB = 128256
MASK_WORDS = 8064
ROWS = 512
PAIRS = 256
DEVICES = 128


def draw_key_cache(key, part):
    key = jax.random.fold_in(key, 11)
    key_base = jax.random.fold_in(key, 0)
    extent = (ROWS, KVH, LMAX, HD)
    base_draw = jnp.clip(jax.random.normal(key_base, extent, jnp.float32), -6.0, 6.0)
    return base_draw.astype(jnp.bfloat16)


def draw_lengths(key, part):
    key = jax.random.fold_in(key, 37)
    key_front, key_back, key_pick = jax.random.split(key, 3)
    leading = jax.random.randint(key_front, (ROWS,), 2, LMAX + 1, dtype=jnp.int32)
    trailing = jax.random.randint(key_back, (ROWS,), 2, LMAX + 1, dtype=jnp.int32)
    skewed = jnp.maximum(leading * trailing // LMAX, 2)
    chosen = jax.random.randint(key_pick, (), 0, ROWS, dtype=jnp.int32)
    return jnp.where(jnp.arange(ROWS, dtype=jnp.int32) == chosen, LMAX, skewed).astype(jnp.int32)


def draw_w_vocab(key, part):
    key = jax.random.fold_in(key, 23)
    key_base, key_scale = jax.random.split(key, 2)
    col_scale = jnp.exp(jax.random.uniform(key_scale, (1, VOCAB), jnp.float32, math.log(0.4), math.log(4.0)))
    base_draw = jnp.clip(jax.random.normal(key_base, (D, VOCAB), jnp.float32), -6.0, 6.0)
    return (base_draw * col_scale * D ** (-0.5)).astype(jnp.bfloat16)


def draw_grammar(key, part):
    key = jax.random.fold_in(key, 53)
    key_one, key_two, key_three, key_depth, key_keep = jax.random.split(key, 5)
    extent = (PAIRS, MASK_WORDS)
    leading = jax.random.randint(key_one, extent, 0, 65536, dtype=jnp.int32)
    middle = jax.random.randint(key_two, extent, 0, 65536, dtype=jnp.int32)
    trailing = jax.random.randint(key_three, extent, 0, 65536, dtype=jnp.int32)
    and_count = jax.random.randint(key_depth, (PAIRS, 1), 0, 3, dtype=jnp.int32)
    packed = leading & jnp.where(and_count >= 1, middle, 65535) & jnp.where(and_count >= 2, trailing, 65535)
    kept_block = (jax.random.randint(key_keep, (PAIRS, DEVICES, 1), 0, 4, dtype=jnp.int32) > 0).astype(jnp.int32)
    return (packed.reshape(PAIRS, DEVICES, WORDS) * kept_block).reshape(PAIRS, MASK_WORDS).astype(jnp.int32)


def block_levels(key, dims, pieces, low, top_value):
    factor_of = 1.0
    for axis_at, parts in pieces:
        steps = jax.random.uniform(jax.random.fold_in(jax.random.fold_in(key, 6), axis_at), (parts,), jnp.float32, low / len(pieces), top_value / len(pieces))
        factor_of = factor_of * jnp.repeat(jnp.exp(steps), dims[axis_at] // parts).reshape((-1,) + (1,) * (len(dims) - 1 - axis_at))
    return factor_of


def noise(key, dims, scale, limit, pieces=(), kind=jnp.bfloat16):
    level = block_levels(key, dims, pieces, -0.22, 0.18) if pieces else 1.0
    drawn = jax.random.normal(key, dims, jnp.float32) * scale * level
    return jnp.minimum(jnp.maximum(drawn, -limit), limit).astype(kind)


def setup_inputs(seed: int = 0) -> dict:
    arg_keys = jax.random.split(jax.random.key(seed), 13)
    return {
        "hidden_in": noise(arg_keys[0], (ROWS, D), 1.0, 6.0, ((1, 32),)),
        "gain_attn": jnp.clip(1.0 + 0.18 * jax.random.normal(arg_keys[1], (D,), jnp.float32), 0.1, 1.9),
        "w_query": noise(arg_keys[2], (D, H * HD), D ** -0.5, 0.0625, ((0, 32), (1, 4))),
        "w_keyval": noise(arg_keys[3], (D, 2, KVH * HD), D ** -0.5, 0.0625, ((0, 32), (2, 4))),
        "w_out": noise(arg_keys[4], (H * HD, D), (H * HD) ** -0.5, 0.0625, ((1, 32),)),
        "key_cache": draw_key_cache(jax.random.fold_in(arg_keys[12], 71), 0),
        "value_cache": noise(arg_keys[6], (ROWS, KVH, LMAX, HD), 1.0, 6.0, ((0, 32), (1, 4))),
        "lengths": draw_lengths(jax.random.fold_in(arg_keys[12], 71), 0),
        "gain_final": jnp.clip(1.0 + 0.18 * jax.random.normal(arg_keys[8], (D,), jnp.float32), 0.1, 1.9),
        "w_vocab": draw_w_vocab(jax.random.fold_in(arg_keys[12], 71), 0),
        "pair_rows": jax.random.permutation(arg_keys[10], ROWS).astype(jnp.int32),
        "grammar": draw_grammar(jax.random.fold_in(arg_keys[12], 71), 0),
    }


GUIDANCE = 3.0
ROPE_BASE = 500000.0
EPSILON = 1e-05
SENTINEL = -1e+30

def rotate(values, positions):
    halves = values.shape[-1] // 2
    frequency = ROPE_BASE ** (-2.0 * jnp.arange(halves, dtype=jnp.float32) / values.shape[-1])
    angles = positions.astype(jnp.float32)[:, None] * frequency[None, :]
    cosine = jnp.cos(angles)[:, None, :]
    sin_part = jnp.sin(angles)[:, None, :]
    leading = values[..., :halves]
    trailing = values[..., halves:]
    return jnp.concatenate([leading * cosine - trailing * sin_part, trailing * cosine + leading * sin_part], -1)

def normalize(stream, gain_vec):
    values = stream.astype(jnp.float32)
    squares = lax.optimization_barrier(jnp.sum(values * values, 1))
    return (values * lax.rsqrt(squares / D + EPSILON)[:, None] * gain_vec[None, :]).astype(jnp.bfloat16)

def unpack(packed, offset, count):
    shifts = jnp.arange(16, dtype=jnp.int32)
    bit_value = jnp.right_shift(packed[:, :, None], shifts[None, None, :]) & 1
    flat_bits = bit_value.reshape(packed.shape[0], -1)[:, :count]
    offsets = jnp.arange(count, dtype=jnp.int32)
    return (flat_bits == 1) | (offset + offsets == 0)[None, :]

def attend(queries, new_key, new_value, key_cache, value_cache, lengths):
    rows, groups = (key_cache.shape[0], key_cache.shape[1])
    group_size = queries.shape[1] // groups
    scaling = queries.shape[2] ** (-0.5)
    grouped = queries.reshape(rows, groups, group_size, -1).astype(jnp.float32)
    scores = jnp.einsum('rgqd,rgld->rgql', grouped, key_cache.astype(jnp.float32)) * scaling
    fresh = jnp.einsum('rgqd,rgd->rgq', grouped, new_key.astype(jnp.float32)) * scaling
    usable = jnp.arange(key_cache.shape[2], dtype=jnp.int32)[None, :] < lengths[:, None]
    scores = jnp.where(usable[:, None, None, :], scores, SENTINEL)
    highest = jnp.maximum(lax.optimization_barrier(jnp.max(scores, -1)), fresh)
    weights = jnp.where(usable[:, None, None, :], jnp.exp(scores - highest[..., None]), 0.0)
    fresh_weight = jnp.exp(fresh - highest)
    summed = lax.optimization_barrier(jnp.sum(weights, -1)) + fresh_weight
    probs_cache = (weights / summed[..., None]).astype(jnp.bfloat16)
    probs_fresh = (fresh_weight / summed).astype(jnp.bfloat16)
    mixed = jnp.einsum('rgql,rgld->rgqd', probs_cache.astype(jnp.float32), value_cache.astype(jnp.float32))
    mixed = mixed + probs_fresh.astype(jnp.float32)[..., None] * new_value.astype(jnp.float32)[:, :, None, :]
    return mixed.reshape(rows, -1).astype(jnp.bfloat16)

def guide(logits, pair_grid):
    cond_rows = logits[pair_grid[:, 0]]
    uncond_rows = logits[pair_grid[:, 1]]
    return uncond_rows + GUIDANCE * (cond_rows - uncond_rows)

def reference(hidden_in, gain_attn, w_query, w_keyval, w_out, key_cache, value_cache, lengths, gain_final, w_vocab, pair_rows, grammar):
    normed = normalize(hidden_in, gain_attn)
    queries = jnp.dot(normed, w_query, preferred_element_type=jnp.float32)
    kv_pairs = jnp.dot(normed, w_keyval.reshape(D, -1), preferred_element_type=jnp.float32).reshape(ROWS, 2, KVH, HD)
    queries = rotate(queries.reshape(ROWS, H, HD), lengths).astype(jnp.bfloat16)
    new_key = rotate(kv_pairs[:, 0], lengths).astype(jnp.bfloat16)
    new_value = kv_pairs[:, 1].astype(jnp.bfloat16)
    attended = attend(queries, new_key, new_value, key_cache, value_cache, lengths)
    update = jnp.dot(attended, w_out, preferred_element_type=jnp.float32)
    residual = (hidden_in.astype(jnp.float32) + update).astype(jnp.bfloat16)
    final_norm = normalize(residual, gain_final).astype(jnp.float32)
    pair_grid = pair_rows.reshape(PAIRS, 2)

    def vocab_block(position):
        columns = lax.dynamic_slice_in_dim(w_vocab, position * V_DEV, V_DEV, 1).astype(jnp.float32)
        logits = jnp.dot(final_norm, columns, precision=lax.Precision.HIGHEST, preferred_element_type=jnp.float32)
        packed = lax.dynamic_slice_in_dim(grammar, position * WORDS, WORDS, 1)
        return (guide(logits, pair_grid), unpack(packed, position * V_DEV, V_DEV))
    guided, allowed = lax.map(vocab_block, jnp.arange(VOCAB // V_DEV, dtype=jnp.int32))
    guided = jnp.moveaxis(guided, 0, 1).reshape(PAIRS, VOCAB)
    allowed = jnp.moveaxis(allowed, 0, 1).reshape(PAIRS, VOCAB)
    masked = jnp.where(allowed, guided, SENTINEL)
    highest = lax.optimization_barrier(jnp.max(masked, 1, keepdims=True))
    summed = lax.optimization_barrier(jnp.sum(jnp.where(allowed, jnp.exp(masked - highest), 0.0), 1, keepdims=True))
    return jnp.where(allowed, guided - highest - jnp.log(summed), 0.0)
```

```python
import functools

import jax
import jax.numpy as jnp
from jax import lax
from jax.experimental import pallas as pl
from jax.experimental.pallas import tpu as pltpu
from jax.sharding import Mesh
from jax.sharding import PartitionSpec as P

D = 8192
HD = 128
NX, NZ, NC, NY = 4, 4, 2, 4
DP = ("x", "z", "c")
ALL = ("x", "z", "c", "y")

GUIDANCE = 3.0
ROPE_BASE = 500000.0
EPSILON = 1e-05
SENTINEL = -1e30
VOCAB_ROWS = 256
WORD_BITS = 16
SHIFTS = (1, 3, 2)
bf16 = jnp.bfloat16
f32 = jnp.float32


def shift(value, axis, by):
    size = lax.axis_size(axis)
    return lax.ppermute(value, axis, [(i, (i + by) % size) for i in range(size)])


def gather_axis(value, axis):
    got = {by: shift(value, axis, by) for by in SHIFTS}
    return jnp.stack([value, got[1], got[2], got[3]])


def rotate(values, cosine, sin_part):
    halves = values.shape[-1] // 2
    leading = values[..., :halves]
    trailing = values[..., halves:]
    return jnp.concatenate(
        [leading * cosine - trailing * sin_part, trailing * cosine + leading * sin_part], -1
    )


def attend(queries, new_key, new_value, key_cache, value_cache, lengths):
    rows, groups = (key_cache.shape[0], key_cache.shape[1])
    group_size = queries.shape[1] // groups
    scaling = queries.shape[2] ** (-0.5)
    grouped = queries.reshape(rows, groups, group_size, -1)
    scores = (
        jnp.einsum("rgqd,rgld->rgql", grouped, key_cache, preferred_element_type=f32)
        * scaling
    )
    fresh = (
        jnp.einsum("rgqd,rgd->rgq", grouped, new_key, preferred_element_type=f32) * scaling
    )
    usable = jnp.arange(key_cache.shape[2], dtype=jnp.int32)[None, :] < lengths[:, None]
    scores = jnp.where(usable[:, None, None, :], scores, SENTINEL)
    highest = jnp.maximum(jnp.max(scores, -1), fresh)
    weights = jnp.where(usable[:, None, None, :], jnp.exp(scores - highest[..., None]), 0.0)
    fresh_weight = jnp.exp(fresh - highest)
    summed = jnp.sum(weights, -1) + fresh_weight
    probs_cache = (weights / summed[..., None]).astype(bf16)
    probs_fresh = (fresh_weight / summed).astype(bf16)
    mixed = jnp.einsum(
        "rgql,rgld->rgqd", probs_cache, value_cache, preferred_element_type=f32
    )
    mixed = (
        mixed
        + probs_fresh.astype(f32)[..., None] * new_value.astype(f32)[:, :, None, :]
    )
    return mixed.reshape(rows, -1).astype(bf16)


def row_total(values, width):
    return values[..., width : width + 1] + values[..., width + 1 : width + 2]


def load_kernel(w_ref, after_ref, out_ref, arrived):
    copy = pltpu.make_async_copy(w_ref, out_ref, arrived)
    copy.start()
    copy.wait()


def load(weights, after, limit):
    hbm = pl.BlockSpec(memory_space=pl.ANY)
    return pl.pallas_call(
        load_kernel,
        out_shape=pltpu.VMEM(weights.shape, weights.dtype),
        in_specs=[hbm, hbm],
        out_specs=pl.BlockSpec(memory_space=pltpu.VMEM),
        scratch_shapes=[pltpu.SemaphoreType.DMA],
        compiler_params=pltpu.CompilerParams(vmem_limit_bytes=limit),
        cost_estimate=pl.CostEstimate(
            flops=0, bytes_accessed=2 * weights.size * weights.dtype.itemsize, transcendentals=0
        ),
    )(weights, after)


def project_kernel(core_ref, hidden_ref, gain_ref, query_ref, keyval_ref, *refs):
    got_ref = refs[0] if len(refs) == 2 else None
    out_ref = refs[-1]
    blocks, _, local_rows, features = hidden_ref.shape
    rows = blocks * local_rows
    values = hidden_ref[:, core_ref[0]].reshape(rows, features).astype(f32)
    total = jnp.sum(values * values, 1, keepdims=True)
    gained = (values * gain_ref[...]).astype(bf16)
    query_cols = query_ref.shape[1]
    width = query_cols + keyval_ref.shape[1]
    extra = out_ref.shape[1] - width

    def put(part, sums):
        if got_ref is not None:
            sums = sums + got_ref[:, part].astype(f32)
        out_ref[:, part] = sums.astype(bf16)

    put(slice(0, query_cols), jnp.dot(gained, query_ref[...], preferred_element_type=f32))
    put(slice(query_cols, width), jnp.dot(gained, keyval_ref[...], preferred_element_type=f32))
    if got_ref is not None:
        parts = got_ref[:, width:].astype(f32)
        total = total + parts[:, 0:1] + parts[:, 1:2]
    high = total.astype(bf16).astype(f32)
    column = lax.broadcasted_iota(jnp.int32, (rows, extra), 1)
    squares = jnp.where(column == 0, high, jnp.where(column == 1, total - high, 0.0))
    out_ref[:, width:] = squares.astype(bf16)


def project(core, hidden, gain, w_query, kv_columns, got):
    blocks, _, local_rows, features = hidden.shape
    rows = blocks * local_rows
    width = w_query.shape[1] + kv_columns.shape[1] + 128
    operands = [hidden, gain, w_query, kv_columns] + ([] if got is None else [got])
    whole = pl.BlockSpec(memory_space=pltpu.VMEM)
    return pl.pallas_call(
        project_kernel,
        out_shape=jax.ShapeDtypeStruct((rows, width), bf16),
        in_specs=[pl.BlockSpec(memory_space=pltpu.SMEM)] + [whole] * len(operands),
        out_specs=whole,
        compiler_params=pltpu.CompilerParams(vmem_limit_bytes=24 * 2**20),
        cost_estimate=pl.CostEstimate(
            flops=2 * rows * width * features, bytes_accessed=4 * rows * width, transcendentals=0
        ),
    )(core.reshape(1).astype(jnp.int32), *operands)


def guide_kernel(scale_ref, *refs):
    out_ref = refs[-1]
    pairs = out_ref.shape[1]
    kept = GUIDANCE * scale_ref[:pairs, :]
    taken = (GUIDANCE - 1.0) * scale_ref[pairs:, :]
    for place, ref in enumerate(refs[:-1]):
        both = kept * ref[:pairs, :].astype(f32) - taken * ref[pairs:, :].astype(f32)
        out_ref[place] = both.astype(bf16)


def guide_pairs(scale, blocks):
    rows, features = blocks[0].shape
    whole = pl.BlockSpec(memory_space=pltpu.VMEM)
    return pl.pallas_call(
        guide_kernel,
        out_shape=jax.ShapeDtypeStruct((len(blocks), rows // 2, features), bf16),
        in_specs=[whole] * (len(blocks) + 1),
        out_specs=whole,
        compiler_params=pltpu.CompilerParams(vmem_limit_bytes=12 * 2**20),
    )(scale, *blocks)


def vocab_kernel(steps, last, *refs):
    places, offset, w_ref = refs[:3]
    held = refs[3 : 3 + steps]
    refs = refs[3 + steps :]
    if last:
        words_ref, acc_ref, out_ref, share_ref = refs
    elif len(refs) == 1:
        (out_ref,) = refs
        acc_ref = None
    else:
        acc_ref, out_ref = refs
    count, pairs = out_ref.shape
    features = held[0].shape[2]
    top = jnp.full((1, pairs), SENTINEL, f32)
    summed = jnp.zeros((1, pairs), f32)
    for first in range(0, count, VOCAB_ROWS):
        rows = min(VOCAB_ROWS, count - first)
        part = slice(first, first + rows)
        total = None if acc_ref is None else acc_ref[part, :]
        for step in range(steps):
            for dz in range(NZ):
                start = pl.multiple_of(places[step * NZ + dz], features)
                product = lax.dot_general(
                    w_ref[part, pl.ds(start, features)],
                    held[step][dz],
                    (((1,), (1,)), ((), ())),
                    preferred_element_type=f32,
                )
                total = product if total is None else total + product
        if not last:
            out_ref[part, :] = total
            continue
        word_rows = -(-rows // WORD_BITS)
        words = words_ref[first // WORD_BITS : first // WORD_BITS + word_rows, :]
        words = jnp.broadcast_to(words[:, None, :], (word_rows, WORD_BITS, pairs))
        words = words.reshape(word_rows * WORD_BITS, pairs)[:rows]
        row = lax.broadcasted_iota(jnp.int32, total.shape, 0)
        bit = lax.shift_right_logical(words, row & (WORD_BITS - 1)) & 1
        allowed = (bit == 1) | (offset[0] + first + row == 0)
        masked = jnp.where(allowed, total, SENTINEL)
        out_ref[part, :] = masked
        before = top
        top = jnp.maximum(before, jnp.max(masked, 0, keepdims=True))
        summed = summed * jnp.exp(before - top) + jnp.sum(
            jnp.where(allowed, jnp.exp(masked - top), 0.0), 0, keepdims=True
        )
    if last:
        share_ref[...] = jnp.where(
            summed > 0.0, top + jnp.log(jnp.maximum(summed, 1e-30)), SENTINEL
        )


def vocab_step(places, offset, w_rows, held, acc, grammar_rows):
    count = w_rows.shape[0]
    pairs, features = held[0].shape[1:]
    depth = len(held) * NZ * features
    last = grammar_rows is not None
    whole = pl.BlockSpec(memory_space=pltpu.VMEM)
    scalars = pl.BlockSpec(memory_space=pltpu.SMEM)
    operands = [w_rows, *held]
    if last:
        operands.append(grammar_rows)
    aliases = {}
    if acc is not None:
        operands.append(acc)
        aliases = {len(operands) + 1: 0}
    out_shape = jax.ShapeDtypeStruct((count, pairs), f32)
    if last:
        out_shape = (out_shape, jax.ShapeDtypeStruct((1, pairs), f32))
    return pl.pallas_call(
        functools.partial(vocab_kernel, len(held), last),
        out_shape=out_shape,
        in_specs=[scalars, scalars] + [whole] * len(operands),
        out_specs=(whole, whole) if last else whole,
        input_output_aliases=aliases,
        compiler_params=pltpu.CompilerParams(vmem_limit_bytes=12 * 2**20),
        cost_estimate=pl.CostEstimate(
            flops=2 * count * pairs * depth, bytes_accessed=2 * count * depth, transcendentals=0
        ),
    )(places, offset, *operands)


def local(
    hidden_in,
    gain_attn,
    w_query,
    w_keyval,
    w_out,
    key_cache,
    value_cache,
    lengths,
    gain_final,
    w_vocab,
    pair_rows,
    grammar,
):
    local_rows = lengths.shape[0]
    row_count, features = hidden_in.shape
    query_cols = w_query.shape[1]
    group_count = w_keyval.shape[2] // HD
    x, z, c, y = (lax.axis_index(axis) for axis in ALL)
    pair_count = row_count // 2

    hidden_blocks = hidden_in.reshape(NX * NZ, NC, local_rows, features)
    gain_row = gain_attn.reshape(1, features)
    kv_columns = w_keyval.reshape(features, -1)
    width = query_cols + kv_columns.shape[1]
    mine = project(1 - c, hidden_blocks, gain_row, w_query, kv_columns, None)
    mine = project(c, hidden_blocks, gain_row, w_query, kv_columns, shift(mine, "c", 1))
    mine = lax.all_to_all(mine.reshape(NX * NZ, local_rows, -1), ("x", "z"), 0, 0)
    mine = jnp.sum(mine.astype(f32), 0)
    projected = mine * lax.rsqrt(row_total(mine, width) / D + EPSILON)

    halves = HD // 2
    frequency = ROPE_BASE ** (-2.0 * jnp.arange(halves, dtype=f32) / HD)
    angles = lengths.astype(f32)[:, None] * frequency[None, :]
    cosine = jnp.cos(angles)[:, None, :]
    sin_part = jnp.sin(angles)[:, None, :]
    queries = rotate(
        projected[:, :query_cols].reshape(local_rows, query_cols // HD, HD), cosine, sin_part
    ).astype(bf16)
    kv_pairs = projected[:, query_cols:width].reshape(local_rows, 2, group_count, HD)
    new_key = rotate(kv_pairs[:, 0], cosine, sin_part).astype(bf16)
    new_value = kv_pairs[:, 1].astype(bf16)
    attended = attend(queries, new_key, new_value, key_cache, value_cache, lengths)

    share = local_rows // NY
    blocks = jnp.broadcast_to(
        attended.reshape(NY, share, query_cols), (NX * NZ, NY, share, query_cols)
    )
    near = lax.all_to_all(blocks.reshape(-1, share, query_cols), ("x", "z", "y"), 0, 0)
    near, weights = lax.optimization_barrier((near, load(w_out, attended, 48 * 2**20)))
    near = near.reshape(NX * NZ, NY, share, query_cols).transpose(0, 2, 1, 3)
    near = near.reshape(NX * NZ * share, D)
    far = shift(near, "c", 1)
    near = jnp.dot(near, weights, preferred_element_type=f32)
    far = jnp.dot(far, weights, preferred_element_type=f32)
    update = jnp.concatenate([jnp.where(c == 0, near, far), jnp.where(c == 0, far, near)], 0)

    hidden_here = lax.dynamic_index_in_dim(
        hidden_in.reshape(NX * NZ, NC, NY, share, features), y, 2, False
    )
    hidden_here = hidden_here.transpose(1, 0, 2, 3).reshape(-1, features)
    residual = (hidden_here.astype(f32) + update).astype(bf16)
    rounded = residual.astype(f32)
    held = residual.shape[0]
    everyone = gather_axis((rounded * gain_final).astype(bf16), "y").reshape(row_count, features)
    quarters = jnp.arange(NY, dtype=jnp.int32)

    def rows_of(order):
        row = (
            jnp.arange(NX * NZ, dtype=jnp.int32)[None, None, :, None] * NC
            + jnp.arange(NC, dtype=jnp.int32)[None, :, None, None]
        ) * local_rows
        row = row + order[:, None, None, None] * share
        return (row + jnp.arange(share, dtype=jnp.int32)).reshape(-1)

    grid = pair_rows.reshape(pair_count, 2).T.reshape(-1, 1)
    pick = (grid == rows_of((y - quarters + NY) % NY)[None, :]).astype(bf16)
    picked = jnp.dot(pick, everyone, preferred_element_type=f32).astype(bf16)
    picked, squares_out = lax.optimization_barrier((picked, jnp.sum(rounded * rounded, 1)))
    shares = lax.all_to_all(
        jnp.broadcast_to(squares_out, (NX * NZ * NC * NY, held)), ALL, 0, 0
    )
    scale = lax.rsqrt(jnp.sum(shares.reshape(-1, NY * held), 0) / D + EPSILON)
    scale = jnp.sum(jnp.where(grid == rows_of(quarters)[None, :], scale[None, :], 0.0), 1)

    got = {by: shift(picked, "z", by) for by in SHIFTS}
    here = guide_pairs(scale[:, None], [picked, got[1], got[2], got[3]])
    sent = {by: shift(here, "x", by) for by in SHIFTS}
    down = jnp.arange(NZ, dtype=jnp.int32)
    offset = lax.axis_index(ALL) * w_vocab.shape[1]
    w_rows = load(w_vocab.T, here, 36 * 2**20)

    def chips(by):
        return ((x - by + NX) % NX) * NZ + (z - down + NZ) % NZ

    def step(blocks, acc, words):
        places = [(chips(by) * NC + (c + far) % NC) * features for by, far, _ in blocks]
        return vocab_step(
            jnp.concatenate(places).astype(jnp.int32),
            offset.reshape(1).astype(jnp.int32),
            w_rows,
            [block for _, _, block in blocks],
            acc,
            words,
        )

    guided = step([(0, 0, here)], None, None)
    guided, here, *arrived = lax.optimization_barrier((guided, here, *(sent[by] for by in SHIFTS)))
    over = [shift(block, "c", 1) for block in (here, *arrived)]
    guided = step(
        [(0, 1, over[0]), (1, 0, arrived[0]), (3, 0, arrived[1]), (2, 0, arrived[2]), (1, 1, over[1])],
        guided,
        None,
    )
    guided = step([(3, 1, over[2]), (2, 1, over[3])], guided, grammar.T)
    masked, shares = guided
    shares = lax.all_to_all(
        jnp.broadcast_to(shares[0], (NX * NZ * NC * NY, pair_count)), ALL, 0, 0
    )
    highest = jnp.max(shares, 0)
    total = highest + jnp.log(jnp.sum(jnp.exp(shares - highest), 0))
    return jnp.where(masked > 0.5 * SENTINEL, masked - total[None, :], 0.0).T


def solution(mesh):
    split = Mesh(mesh.devices.reshape(NX, NZ, NC, NY), ALL)
    in_specs = (
        P(None, DP),
        P(DP),
        P(DP, "y"),
        P(DP, None, "y"),
        P(None, DP),
        P(DP, "y", None, None),
        P(DP, "y", None, None),
        P(DP),
        P(DP),
        P(None, ALL),
        P(),
        P(None, ALL),
    )
    out_specs = P(None, ALL)
    return jax.shard_map(local, mesh=split, in_specs=in_specs, out_specs=out_specs, check_vma=False)
```

```python
import functools

import jax
import jax.numpy as jnp
from jax import lax
from jax.experimental import pallas as pl
from jax.experimental.pallas import tpu as pltpu
from jax.sharding import Mesh
from jax.sharding import PartitionSpec as P

D = 8192
HD = 128
NX, NZ, NC, NY = 4, 4, 2, 4
DP = ("x", "z", "c")
ALL = ("x", "z", "c", "y")

GUIDANCE = 3.0
ROPE_BASE = 500000.0
EPSILON = 1e-05
SENTINEL = -1e30
VOCAB_ROWS = 256
WORD_BITS = 16
SHIFTS = (1, 3, 2)
SWAPS = (("x", 1), ("x", 3), ("z", 1), ("z", 3))
PARTS = len(SWAPS)
bf16 = jnp.bfloat16
f32 = jnp.float32


def shift(value, axis, by):
    size = lax.axis_size(axis)
    return lax.ppermute(value, axis, [(i, (i + by) % size) for i in range(size)])


def swap(value, part, step):
    axis, by = SWAPS[(part + step) % PARTS]
    return lax.ppermute(value, axis, [(i, i ^ by) for i in range(lax.axis_size(axis))])


def slot_of(part, distance):
    return sum((distance >> (part + step) % PARTS & 1) << step for step in range(PARTS))


def rotate(values, cosine, sin_part):
    halves = values.shape[-1] // 2
    leading = values[..., :halves]
    trailing = values[..., halves:]
    return jnp.concatenate(
        [leading * cosine - trailing * sin_part, trailing * cosine + leading * sin_part], -1
    )


def attend(queries, new_key, new_value, key_cache, value_cache, lengths):
    rows, groups = (key_cache.shape[0], key_cache.shape[1])
    group_size = queries.shape[1] // groups
    scaling = queries.shape[2] ** (-0.5)
    grouped = queries.reshape(rows, groups, group_size, -1)
    scores = (
        jnp.einsum("rgqd,rgld->rgql", grouped, key_cache, preferred_element_type=f32)
        * scaling
    )
    fresh = (
        jnp.einsum("rgqd,rgd->rgq", grouped, new_key, preferred_element_type=f32) * scaling
    )
    usable = jnp.arange(key_cache.shape[2], dtype=jnp.int32)[None, :] < lengths[:, None]
    scores = jnp.where(usable[:, None, None, :], scores, SENTINEL)
    highest = jnp.maximum(jnp.max(scores, -1), fresh)
    weights = jnp.where(usable[:, None, None, :], jnp.exp(scores - highest[..., None]), 0.0)
    fresh_weight = jnp.exp(fresh - highest)
    summed = jnp.sum(weights, -1) + fresh_weight
    probs_cache = (weights / summed[..., None]).astype(bf16)
    probs_fresh = (fresh_weight / summed).astype(bf16)
    mixed = jnp.einsum(
        "rgql,rgld->rgqd", probs_cache, value_cache, preferred_element_type=f32
    )
    mixed = (
        mixed
        + probs_fresh.astype(f32)[..., None] * new_value.astype(f32)[:, :, None, :]
    )
    return mixed.reshape(rows, -1).astype(bf16)


def row_total(values, width):
    return values[..., width : width + 1] + values[..., width + 1 : width + 2]


def small_cost(flops, moved):
    return pl.CostEstimate(flops=flops, bytes_accessed=moved, transcendentals=0)


def load_kernel(w_ref, after_ref, out_ref, arrived):
    copy = pltpu.make_async_copy(w_ref, out_ref, arrived)
    copy.start()
    copy.wait()


def load(weights, after, limit):
    hbm = pl.BlockSpec(memory_space=pl.ANY)
    return pl.pallas_call(
        load_kernel,
        out_shape=pltpu.VMEM(weights.shape, weights.dtype),
        in_specs=[hbm, hbm],
        out_specs=pl.BlockSpec(memory_space=pltpu.VMEM),
        scratch_shapes=[pltpu.SemaphoreType.DMA],
        compiler_params=pltpu.CompilerParams(vmem_limit_bytes=limit),
        cost_estimate=pl.CostEstimate(
            flops=0, bytes_accessed=2 * weights.size * weights.dtype.itemsize, transcendentals=0
        ),
    )(weights, after)


def repeat_kernel(block_ref, out_ref):
    for copy in range(out_ref.shape[0]):
        out_ref[copy] = block_ref[...]


def repeat(block, copies):
    whole = pl.BlockSpec(memory_space=pltpu.VMEM)
    return pl.pallas_call(
        repeat_kernel,
        out_shape=jax.ShapeDtypeStruct((copies,) + block.shape, block.dtype),
        in_specs=[whole],
        out_specs=whole,
        compiler_params=pltpu.CompilerParams(vmem_limit_bytes=12 * 2**20),
        cost_estimate=small_cost(0, 2 * (copies + 1) * block.size),
    )(block)


def project_kernel(core_ref, hidden_ref, gain_ref, query_ref, keyval_ref, *refs):
    got_ref = refs[0] if len(refs) == 2 else None
    out_ref = refs[-1]
    blocks, _, local_rows, features = hidden_ref.shape
    rows = blocks * local_rows
    values = hidden_ref[:, core_ref[0]].reshape(rows, features).astype(f32)
    total = jnp.sum(values * values, 1, keepdims=True)
    gained = (values * gain_ref[...]).astype(bf16)
    query_cols = query_ref.shape[1]
    key_cols = keyval_ref.shape[2]
    width = query_cols + 2 * key_cols
    extra = out_ref.shape[1] - width

    def put(part, sums):
        if got_ref is not None:
            sums = sums + got_ref[:, part].astype(f32)
        out_ref[:, part] = sums.astype(bf16)

    put(slice(0, query_cols), jnp.dot(gained, query_ref[...], preferred_element_type=f32))
    for half in range(2):
        start = query_cols + half * key_cols
        sums = jnp.dot(gained, keyval_ref[:, half, :], preferred_element_type=f32)
        put(slice(start, start + key_cols), sums)
    if got_ref is not None:
        parts = got_ref[:, width:].astype(f32)
        total = total + parts[:, 0:1] + parts[:, 1:2]
    high = total.astype(bf16).astype(f32)
    column = lax.broadcasted_iota(jnp.int32, (rows, extra), 1)
    squares = jnp.where(column == 0, high, jnp.where(column == 1, total - high, 0.0))
    out_ref[:, width:] = squares.astype(bf16)


def project(core, hidden, gain, w_query, w_keyval, got, limit):
    blocks, _, local_rows, features = hidden.shape
    rows = blocks * local_rows
    width = w_query.shape[1] + w_keyval.shape[1] * w_keyval.shape[2] + 128
    operands = [hidden, gain, w_query, w_keyval] + ([] if got is None else [got])
    whole = pl.BlockSpec(memory_space=pltpu.VMEM)
    return pl.pallas_call(
        project_kernel,
        out_shape=jax.ShapeDtypeStruct((rows, width), bf16),
        in_specs=[pl.BlockSpec(memory_space=pltpu.SMEM)] + [whole] * len(operands),
        out_specs=whole,
        compiler_params=pltpu.CompilerParams(vmem_limit_bytes=limit * 2**20),
        cost_estimate=pl.CostEstimate(
            flops=2 * rows * width * features, bytes_accessed=4 * rows * width, transcendentals=0
        ),
    )(core.reshape(1).astype(jnp.int32), *operands)


def pick_kernel(pick_ref, *refs):
    blocks, outs = refs[:NY], refs[NY:]
    held = blocks[0].shape[0]
    rows = outs[0].shape[1]
    for part, out_ref in enumerate(outs):
        lines = slice(part * rows, (part + 1) * rows)
        total = None
        for quarter, block in enumerate(blocks):
            chosen = pick_ref[lines, quarter * held : (quarter + 1) * held]
            product = jnp.dot(chosen, block[...], preferred_element_type=f32)
            total = product if total is None else total + product
        out_ref[0] = total.astype(bf16)


def pick_rows(pick, blocks):
    whole = pl.BlockSpec(memory_space=pltpu.VMEM)
    shape = (1, pick.shape[0] // PARTS, blocks[0].shape[1])
    return pl.pallas_call(
        pick_kernel,
        out_shape=[jax.ShapeDtypeStruct(shape, bf16)] * PARTS,
        in_specs=[whole] * (1 + len(blocks)),
        out_specs=[whole] * PARTS,
        compiler_params=pltpu.CompilerParams(vmem_limit_bytes=12 * 2**20),
        cost_estimate=small_cost(2 * pick.size * blocks[0].shape[1], pick.size * 4),
    )(pick, *blocks)


def join_kernel(*refs):
    ins, outs = refs[: 2 * PARTS], refs[2 * PARTS :]
    count = ins[0].shape[0]
    for part in range(PARTS):
        for half in range(2):
            value = ins[2 * part + half][...]
            lines = slice(half * count, (half + 1) * count)
            outs[part][lines] = value
            if len(outs) > PARTS:
                outs[PARTS][part, lines] = value


def join(pairs, together):
    whole = pl.BlockSpec(memory_space=pltpu.VMEM)
    count, *rest = pairs[0][0].shape
    shapes = [jax.ShapeDtypeStruct((2 * count, *rest), bf16)] * PARTS
    if together:
        shapes.append(jax.ShapeDtypeStruct((PARTS, 2 * count, *rest), bf16))
    return pl.pallas_call(
        join_kernel,
        out_shape=shapes,
        in_specs=[whole] * (2 * PARTS),
        out_specs=[whole] * len(shapes),
        compiler_params=pltpu.CompilerParams(vmem_limit_bytes=12 * 2**20),
        cost_estimate=small_cost(0, 16 * PARTS * pairs[0][0].size),
    )(*(half for pair in pairs for half in pair))


def guide_kernel(shares_ref, place_ref, *refs):
    ins, outs = refs[: 2 * PARTS], refs[2 * PARTS :]
    devices, held = shares_ref.shape
    total = jnp.sum(shares_ref[...].reshape(devices // NY, NY, held), 0)
    scale = lax.rsqrt(total / D + EPSILON)
    place = place_ref[...]
    lane = lax.broadcasted_iota(jnp.int32, (place.shape[0], held), 1)
    chosen = jnp.zeros((place.shape[0], held), f32)
    for quarter in range(NY):
        here = lane + quarter * held == place
        chosen = chosen + jnp.where(here, scale[quarter : quarter + 1, :], 0.0)
    chosen = jnp.sum(chosen, 1, keepdims=True)
    rows = ins[0].shape[1]
    half = rows // 2
    for part in range(PARTS):
        kept = GUIDANCE * chosen[part * rows : part * rows + half]
        taken = (GUIDANCE - 1.0) * chosen[part * rows + half : (part + 1) * rows]
        for slot in range(outs[part].shape[0]):
            ref = ins[2 * part + slot // 2]
            both = kept * ref[slot % 2, :half, :].astype(f32)
            both = both - taken * ref[slot % 2, half:, :].astype(f32)
            outs[part][slot] = both.astype(bf16)


def guide_pairs(shares, place, pairs):
    _, rows, features = pairs[0][0].shape
    whole = pl.BlockSpec(memory_space=pltpu.VMEM)
    return pl.pallas_call(
        guide_kernel,
        out_shape=[jax.ShapeDtypeStruct((4, rows // 2, features), bf16)] * PARTS,
        in_specs=[whole] * (2 + 2 * PARTS),
        out_specs=[whole] * PARTS,
        compiler_params=pltpu.CompilerParams(vmem_limit_bytes=12 * 2**20),
        cost_estimate=small_cost(0, 16 * PARTS * pairs[0][0].size),
    )(shares, place, *(half for pair in pairs for half in pair))


def vocab_kernel(count, places, w_ref, *refs):
    near, far, near_later, far_later = (
        refs[:PARTS],
        refs[PARTS],
        refs[PARTS + 1 : 2 * PARTS + 1],
        refs[2 * PARTS + 1 : 3 * PARTS + 1],
    )
    words_ref, out_ref, share_ref, top_ref, sum_ref = refs[3 * PARTS + 1 :]
    features = near[0].shape[2]
    early = near[0].shape[0]

    def piece(core, part, slot):
        if slot >= early:
            return (far_later if core else near_later)[part][slot - early]
        return far[part, slot] if core else near[part][slot]

    total = None
    for core in range(NC):
        for distance in range(NX * NZ):
            start = pl.multiple_of(places[1 + core * NX * NZ + distance], features)
            held = [piece(core, part, slot_of(part, distance)) for part in range(PARTS)]
            product = lax.dot_general(
                w_ref[:, pl.ds(start, features)],
                jnp.concatenate(held, 0),
                (((1,), (1,)), ((), ())),
                preferred_element_type=f32,
            )
            total = product if total is None else total + product
    step = pl.program_id(0)
    rows, pairs = total.shape
    words = words_ref[...]
    words = jnp.broadcast_to(words[:, None, :], (words.shape[0], WORD_BITS, pairs))
    words = words.reshape(rows, pairs)
    row = lax.broadcasted_iota(jnp.int32, total.shape, 0)
    place = step * rows + row
    bit = lax.shift_right_logical(words, row & (WORD_BITS - 1)) & 1
    allowed = ((bit == 1) | (places[0] + place == 0)) & (place < count)
    masked = jnp.where(allowed, total, SENTINEL)
    out_ref[...] = masked

    @pl.when(step == 0)
    def _():
        top_ref[...] = jnp.full_like(top_ref, SENTINEL)
        sum_ref[...] = jnp.zeros_like(sum_ref)

    before = top_ref[...]
    top = jnp.maximum(before, jnp.max(masked, 0, keepdims=True))
    summed = sum_ref[...] * jnp.exp(before - top) + jnp.sum(
        jnp.where(allowed, jnp.exp(masked - top), 0.0), 0, keepdims=True
    )
    top_ref[...] = top
    sum_ref[...] = summed

    @pl.when(step == pl.num_programs(0) - 1)
    def _():
        share_ref[...] = jnp.where(
            summed > 0.0, top + jnp.log(jnp.maximum(summed, 1e-30)), SENTINEL
        )


def vocab_logits(places, w_rows, near, far, near_later, far_later, grammar_rows):
    count, depth = w_rows.shape
    pairs = PARTS * near[0].shape[1]
    blocks = [*near, far, *near_later, *far_later]

    def whole(block):
        return pl.BlockSpec(
            block.shape, lambda i, s: (0,) * block.ndim, pipeline_mode=pl.Buffered(1)
        )

    part = pl.BlockSpec((VOCAB_ROWS, pairs), lambda i, s: (i, 0))
    return pl.pallas_call(
        functools.partial(vocab_kernel, count),
        out_shape=(
            jax.ShapeDtypeStruct((count, pairs), f32),
            jax.ShapeDtypeStruct((1, pairs), f32),
        ),
        grid_spec=pltpu.PrefetchScalarGridSpec(
            num_scalar_prefetch=1,
            grid=(pl.cdiv(count, VOCAB_ROWS),),
            in_specs=[
                pl.BlockSpec((VOCAB_ROWS, depth), lambda i, s: (i, 0)),
                *(whole(block) for block in blocks),
                pl.BlockSpec((VOCAB_ROWS // WORD_BITS, pairs), lambda i, s: (i, 0)),
            ],
            out_specs=(part, pl.BlockSpec((1, pairs), lambda i, s: (0, 0))),
            scratch_shapes=[pltpu.VMEM((1, pairs), f32), pltpu.VMEM((1, pairs), f32)],
        ),
        compiler_params=pltpu.CompilerParams(vmem_limit_bytes=48 * 2**20),
        cost_estimate=pl.CostEstimate(
            flops=2 * count * pairs * depth, bytes_accessed=2 * count * depth, transcendentals=0
        ),
    )(places, w_rows, *blocks, grammar_rows)


def local(
    hidden_in,
    gain_attn,
    w_query,
    w_keyval,
    w_out,
    key_cache,
    value_cache,
    lengths,
    gain_final,
    w_vocab,
    pair_rows,
    grammar,
):
    local_rows = lengths.shape[0]
    row_count, features = hidden_in.shape
    query_cols = w_query.shape[1]
    group_count = w_keyval.shape[2] // HD
    x, z, c, y = (lax.axis_index(axis) for axis in ALL)
    pair_count = row_count // 2

    hidden_blocks = hidden_in.reshape(NX * NZ, NC, local_rows, features)
    gain_row = gain_attn.reshape(1, features)
    width = query_cols + w_keyval.shape[1] * w_keyval.shape[2]
    mine = project(1 - c, hidden_blocks, gain_row, w_query, w_keyval, None, 56)
    mine = project(c, hidden_blocks, gain_row, w_query, w_keyval, shift(mine, "c", 1), 24)
    mine = lax.all_to_all(mine.reshape(NX * NZ, local_rows, -1), ("x", "z"), 0, 0)
    mine = jnp.sum(mine.astype(f32), 0)
    projected = mine * lax.rsqrt(row_total(mine, width) / D + EPSILON)

    halves = HD // 2
    frequency = ROPE_BASE ** (-2.0 * jnp.arange(halves, dtype=f32) / HD)
    angles = lengths.astype(f32)[:, None] * frequency[None, :]
    cosine = jnp.cos(angles)[:, None, :]
    sin_part = jnp.sin(angles)[:, None, :]
    queries = rotate(
        projected[:, :query_cols].reshape(local_rows, query_cols // HD, HD), cosine, sin_part
    ).astype(bf16)
    kv_pairs = projected[:, query_cols:width].reshape(local_rows, 2, group_count, HD)
    new_key = rotate(kv_pairs[:, 0], cosine, sin_part).astype(bf16)
    new_value = kv_pairs[:, 1].astype(bf16)
    attended = attend(queries, new_key, new_value, key_cache, value_cache, lengths)

    share = local_rows // NY
    blocks = repeat(attended.reshape(NY, share, query_cols), NX * NZ)
    near = lax.all_to_all(blocks.reshape(-1, share, query_cols), ("x", "z", "y"), 0, 0)
    near, weights = lax.optimization_barrier((near, load(w_out, attended, 48 * 2**20)))
    near = near.reshape(NX * NZ, NY, share, query_cols).transpose(0, 2, 1, 3)
    near = near.reshape(NX * NZ * share, D)
    far = shift(near, "c", 1)
    near = jnp.dot(near, weights, preferred_element_type=f32)
    far = jnp.dot(far, weights, preferred_element_type=f32)
    update = jnp.concatenate([jnp.where(c == 0, near, far), jnp.where(c == 0, far, near)], 0)

    hidden_here = lax.dynamic_index_in_dim(
        hidden_in.reshape(NX * NZ, NC, NY, share, features), y, 2, False
    )
    hidden_here = hidden_here.transpose(1, 0, 2, 3).reshape(-1, features)
    residual = (hidden_here.astype(f32) + update).astype(bf16)
    rounded = residual.astype(f32)
    held = residual.shape[0]
    scaled = (rounded * gain_final).astype(bf16)
    got = {by: shift(scaled, "y", by) for by in SHIFTS}
    quarters = jnp.arange(NY, dtype=jnp.int32)

    def rows_of(order):
        row = (
            jnp.arange(NX * NZ, dtype=jnp.int32)[None, None, :, None] * NC
            + jnp.arange(NC, dtype=jnp.int32)[None, :, None, None]
        ) * local_rows
        row = row + order[:, None, None, None] * share
        return (row + jnp.arange(share, dtype=jnp.int32)).reshape(-1)

    grid = pair_rows.reshape(PARTS, pair_count // PARTS, 2).transpose(0, 2, 1).reshape(-1, 1)
    pick = (grid == rows_of((y - quarters + NY) % NY)[None, :]).astype(bf16)
    order = jnp.arange(row_count, dtype=jnp.int32)
    place = jnp.sum(jnp.where(grid == rows_of(quarters)[None, :], order[None, :], 0), 1)

    parts = pick_rows(pick, [scaled, got[1], got[2], got[3]])
    shares = lax.all_to_all(
        jnp.broadcast_to(jnp.sum(rounded * rounded, 1), (NX * NZ * NC * NY, held)), ALL, 0, 0
    )
    parts = join([(part, swap(part, i, 0)) for i, part in enumerate(parts)], False)
    parts = [(part, swap(part, i, 1)) for i, part in enumerate(parts)]
    shares, first = lax.optimization_barrier((shares, parts[0][1]))
    parts[0] = (parts[0][0], first)
    parts = guide_pairs(shares, place[:, None], parts)
    *near, together = join([(part, swap(part, i, 2)) for i, part in enumerate(parts)], True)
    far = shift(together, "c", 1)
    near_later = [swap(part, i, 3) for i, part in enumerate(near)]
    far_later = [shift(part, "c", 1) for part in near_later]

    columns = []
    for core in range(NC):
        for distance in range(NX * NZ):
            where = {"x": x, "z": z}
            for bit, (axis, by) in enumerate(SWAPS):
                if distance >> bit & 1:
                    where[axis] = where[axis] ^ by
            columns.append(((where["x"] * NZ + where["z"]) * NC + (c + core) % NC) * features)
    offset = lax.axis_index(ALL) * w_vocab.shape[1]
    guided = vocab_logits(
        jnp.stack([offset, *columns]).astype(jnp.int32),
        w_vocab.T,
        near,
        far,
        near_later,
        far_later,
        grammar.T,
    )
    masked, shares = guided
    shares = lax.all_to_all(
        jnp.broadcast_to(shares[0], (NX * NZ * NC * NY, pair_count)), ALL, 0, 0
    )
    highest = jnp.max(shares, 0)
    total = highest + jnp.log(jnp.sum(jnp.exp(shares - highest), 0))
    return jnp.where(masked > 0.5 * SENTINEL, masked - total[None, :], 0.0).T


def solution(mesh):
    split = Mesh(mesh.devices.reshape(NX, NZ, NC, NY), ALL)
    in_specs = (
        P(None, DP),
        P(DP),
        P(DP, "y"),
        P(DP, None, "y"),
        P(None, DP),
        P(DP, "y", None, None),
        P(DP, "y", None, None),
        P(DP),
        P(DP),
        P(None, ALL),
        P(),
        P(None, ALL),
    )
    out_specs = P(None, ALL)
    return jax.shard_map(local, mesh=split, in_specs=in_specs, out_specs=out_specs, check_vma=False)
```

```python
import functools

import jax
import jax.numpy as jnp
from jax import lax
from jax.experimental import pallas as pl
from jax.experimental.pallas import tpu as pltpu
from jax.sharding import Mesh
from jax.sharding import PartitionSpec as P

D = 8192
HD = 128
NX, NZ, NC, NY = 4, 4, 2, 4
DP = ("x", "z", "c")
ALL = ("x", "z", "c", "y")

GUIDANCE = 3.0
ROPE_BASE = 500000.0
EPSILON = 1e-05
SENTINEL = -1e30
VOCAB_ROWS = 256
WORD_BITS = 16
SHIFTS = (1, 3, 2)
SWAPS = (("x", 1), ("x", 3), ("z", 1), ("z", 3))
PARTS = len(SWAPS)
SQUARES_COPIES = 4
bf16 = jnp.bfloat16
f32 = jnp.float32


def shift(value, axis, by):
    size = lax.axis_size(axis)
    return lax.ppermute(value, axis, [(i, (i + by) % size) for i in range(size)])


def swap(value, part, step):
    axis, by = SWAPS[(part + step) % PARTS]
    return lax.ppermute(value, axis, [(i, i ^ by) for i in range(lax.axis_size(axis))])


def slot_of(part, distance):
    return sum((distance >> (part + step) % PARTS & 1) << step for step in range(PARTS))


def rotate(values, cosine, sin_part):
    halves = values.shape[-1] // 2
    leading = values[..., :halves]
    trailing = values[..., halves:]
    return jnp.concatenate(
        [leading * cosine - trailing * sin_part, trailing * cosine + leading * sin_part], -1
    )


def attend(queries, new_key, new_value, key_cache, value_cache, lengths):
    rows, groups = (key_cache.shape[0], key_cache.shape[1])
    group_size = queries.shape[1] // groups
    scaling = queries.shape[2] ** (-0.5)
    grouped = queries.reshape(rows, groups, group_size, -1)
    scores = (
        jnp.einsum("rgqd,rgld->rgql", grouped, key_cache, preferred_element_type=f32)
        * scaling
    )
    fresh = (
        jnp.einsum("rgqd,rgd->rgq", grouped, new_key, preferred_element_type=f32) * scaling
    )
    usable = jnp.arange(key_cache.shape[2], dtype=jnp.int32)[None, :] < lengths[:, None]
    scores = jnp.where(usable[:, None, None, :], scores, SENTINEL)
    highest = jnp.maximum(jnp.max(scores, -1), fresh)
    weights = jnp.where(usable[:, None, None, :], jnp.exp(scores - highest[..., None]), 0.0)
    fresh_weight = jnp.exp(fresh - highest)
    summed = jnp.sum(weights, -1) + fresh_weight
    probs_cache = (weights / summed[..., None]).astype(bf16)
    probs_fresh = (fresh_weight / summed).astype(bf16)
    mixed = jnp.einsum(
        "rgql,rgld->rgqd", probs_cache, value_cache, preferred_element_type=f32
    )
    mixed = (
        mixed
        + probs_fresh.astype(f32)[..., None] * new_value.astype(f32)[:, :, None, :]
    )
    return mixed.reshape(rows, -1).astype(bf16)


def row_total(values, width):
    return values[..., width : width + 1] + values[..., width + 1 : width + 2]


def small_cost(flops, moved):
    return pl.CostEstimate(flops=flops, bytes_accessed=moved, transcendentals=0)


def load_kernel(w_ref, after_ref, out_ref, arrived):
    copy = pltpu.make_async_copy(w_ref, out_ref, arrived)
    copy.start()
    copy.wait()


def load(weights, after, limit):
    hbm = pl.BlockSpec(memory_space=pl.ANY)
    return pl.pallas_call(
        load_kernel,
        out_shape=pltpu.VMEM(weights.shape, weights.dtype),
        in_specs=[hbm, hbm],
        out_specs=pl.BlockSpec(memory_space=pltpu.VMEM),
        scratch_shapes=[pltpu.SemaphoreType.DMA],
        compiler_params=pltpu.CompilerParams(vmem_limit_bytes=limit),
        cost_estimate=pl.CostEstimate(
            flops=0, bytes_accessed=2 * weights.size * weights.dtype.itemsize, transcendentals=0
        ),
    )(weights, after)


def repeat_kernel(block_ref, out_ref):
    for copy in range(out_ref.shape[0]):
        out_ref[copy] = block_ref[...]


def repeat(block, copies):
    whole = pl.BlockSpec(memory_space=pltpu.VMEM)
    return pl.pallas_call(
        repeat_kernel,
        out_shape=jax.ShapeDtypeStruct((copies,) + block.shape, block.dtype),
        in_specs=[whole],
        out_specs=whole,
        compiler_params=pltpu.CompilerParams(vmem_limit_bytes=12 * 2**20),
        cost_estimate=small_cost(0, 2 * (copies + 1) * block.size),
    )(block)


def project_kernel(core_ref, hidden_ref, gain_ref, query_ref, keyval_ref, *refs):
    got_ref = refs[0] if len(refs) == 2 else None
    out_ref = refs[-1]
    blocks, _, local_rows, features = hidden_ref.shape
    rows = blocks * local_rows
    values = hidden_ref[:, core_ref[0]].reshape(rows, features).astype(f32)
    total = jnp.sum(values * values, 1, keepdims=True)
    gained = (values * gain_ref[...]).astype(bf16)
    query_cols = query_ref.shape[1]
    key_cols = keyval_ref.shape[2]
    width = query_cols + 2 * key_cols
    extra = out_ref.shape[1] - width

    def put(part, sums):
        if got_ref is not None:
            sums = sums + got_ref[:, part].astype(f32)
        out_ref[:, part] = sums.astype(bf16)

    put(slice(0, query_cols), jnp.dot(gained, query_ref[...], preferred_element_type=f32))
    for half in range(2):
        start = query_cols + half * key_cols
        sums = jnp.dot(gained, keyval_ref[:, half, :], preferred_element_type=f32)
        put(slice(start, start + key_cols), sums)
    if got_ref is not None:
        parts = got_ref[:, width:].astype(f32)
        total = total + parts[:, 0:1] + parts[:, 1:2]
    high = total.astype(bf16).astype(f32)
    column = lax.broadcasted_iota(jnp.int32, (rows, extra), 1)
    squares = jnp.where(column == 0, high, jnp.where(column == 1, total - high, 0.0))
    out_ref[:, width:] = squares.astype(bf16)


def project(core, hidden, gain, w_query, w_keyval, got, limit):
    blocks, _, local_rows, features = hidden.shape
    rows = blocks * local_rows
    width = w_query.shape[1] + w_keyval.shape[1] * w_keyval.shape[2] + 128
    operands = [hidden, gain, w_query, w_keyval] + ([] if got is None else [got])
    whole = pl.BlockSpec(memory_space=pltpu.VMEM)
    return pl.pallas_call(
        project_kernel,
        out_shape=jax.ShapeDtypeStruct((rows, width), bf16),
        in_specs=[pl.BlockSpec(memory_space=pltpu.SMEM)] + [whole] * len(operands),
        out_specs=whole,
        compiler_params=pltpu.CompilerParams(vmem_limit_bytes=limit * 2**20),
        cost_estimate=pl.CostEstimate(
            flops=2 * rows * width * features, bytes_accessed=4 * rows * width, transcendentals=0
        ),
    )(core.reshape(1).astype(jnp.int32), *operands)


def pick_kernel(pick_ref, *refs):
    blocks, outs = refs[:NY], refs[NY:]
    held = blocks[0].shape[0]
    rows = outs[0].shape[1]
    for part, out_ref in enumerate(outs):
        lines = slice(part * rows, (part + 1) * rows)
        total = None
        for quarter, block in enumerate(blocks):
            chosen = pick_ref[lines, quarter * held : (quarter + 1) * held]
            product = jnp.dot(chosen, block[...], preferred_element_type=f32)
            total = product if total is None else total + product
        out_ref[0] = total.astype(bf16)


def pick_rows(pick, blocks):
    whole = pl.BlockSpec(memory_space=pltpu.VMEM)
    shape = (1, pick.shape[0] // PARTS, blocks[0].shape[1])
    return pl.pallas_call(
        pick_kernel,
        out_shape=[jax.ShapeDtypeStruct(shape, bf16)] * PARTS,
        in_specs=[whole] * (1 + len(blocks)),
        out_specs=[whole] * PARTS,
        compiler_params=pltpu.CompilerParams(vmem_limit_bytes=12 * 2**20),
        cost_estimate=small_cost(2 * pick.size * blocks[0].shape[1], pick.size * 4),
    )(pick, *blocks)


def join_kernel(*refs):
    ins, outs = refs[: 2 * PARTS], refs[2 * PARTS :]
    count = ins[0].shape[0]
    for part in range(PARTS):
        for half in range(2):
            value = ins[2 * part + half][...]
            lines = slice(half * count, (half + 1) * count)
            outs[part][lines] = value
            if len(outs) > PARTS:
                outs[PARTS][part, lines] = value


def join(pairs, together):
    whole = pl.BlockSpec(memory_space=pltpu.VMEM)
    count, *rest = pairs[0][0].shape
    shapes = [jax.ShapeDtypeStruct((2 * count, *rest), bf16)] * PARTS
    if together:
        shapes.append(jax.ShapeDtypeStruct((PARTS, 2 * count, *rest), bf16))
    return pl.pallas_call(
        join_kernel,
        out_shape=shapes,
        in_specs=[whole] * (2 * PARTS),
        out_specs=[whole] * len(shapes),
        compiler_params=pltpu.CompilerParams(vmem_limit_bytes=12 * 2**20),
        cost_estimate=small_cost(0, 16 * PARTS * pairs[0][0].size),
    )(*(half for pair in pairs for half in pair))


def guide_kernel(shares_ref, place_ref, *refs):
    ins, outs = refs[: 2 * PARTS], refs[2 * PARTS :]
    devices, held = shares_ref.shape
    total = jnp.sum(shares_ref[...].reshape(devices // NY, NY, held), 0)
    scale = lax.rsqrt(total / D + EPSILON)
    place = place_ref[...]
    lane = lax.broadcasted_iota(jnp.int32, (place.shape[0], held), 1)
    chosen = jnp.zeros((place.shape[0], held), f32)
    for quarter in range(NY):
        here = lane + quarter * held == place
        chosen = chosen + jnp.where(here, scale[quarter : quarter + 1, :], 0.0)
    chosen = jnp.sum(chosen, 1, keepdims=True)
    rows = ins[0].shape[1]
    half = rows // 2
    for part in range(PARTS):
        kept = GUIDANCE * chosen[part * rows : part * rows + half]
        taken = (GUIDANCE - 1.0) * chosen[part * rows + half : (part + 1) * rows]
        for slot in range(outs[part].shape[0]):
            ref = ins[2 * part + slot // 2]
            both = kept * ref[slot % 2, :half, :].astype(f32)
            both = both - taken * ref[slot % 2, half:, :].astype(f32)
            outs[part][slot] = both.astype(bf16)


def guide_pairs(shares, place, pairs):
    _, rows, features = pairs[0][0].shape
    whole = pl.BlockSpec(memory_space=pltpu.VMEM)
    return pl.pallas_call(
        guide_kernel,
        out_shape=[jax.ShapeDtypeStruct((4, rows // 2, features), bf16)] * PARTS,
        in_specs=[whole] * (2 + 2 * PARTS),
        out_specs=[whole] * PARTS,
        compiler_params=pltpu.CompilerParams(vmem_limit_bytes=12 * 2**20),
        cost_estimate=small_cost(0, 16 * PARTS * pairs[0][0].size),
    )(shares, place, *(half for pair in pairs for half in pair))


def vocab_kernel(count, places, w_ref, *refs):
    near, far, near_later, far_later = (
        refs[:PARTS],
        refs[PARTS],
        refs[PARTS + 1 : 2 * PARTS + 1],
        refs[2 * PARTS + 1 : 3 * PARTS + 1],
    )
    words_ref, out_ref, share_ref, top_ref, sum_ref = refs[3 * PARTS + 1 :]
    features = near[0].shape[2]
    early = near[0].shape[0]

    def piece(core, part, slot):
        if slot >= early:
            return (far_later if core else near_later)[part][slot - early]
        return far[part, slot] if core else near[part][slot]

    total = None
    for core in range(NC):
        for distance in range(NX * NZ):
            start = pl.multiple_of(places[1 + core * NX * NZ + distance], features)
            held = [piece(core, part, slot_of(part, distance)) for part in range(PARTS)]
            product = lax.dot_general(
                w_ref[:, pl.ds(start, features)],
                jnp.concatenate(held, 0),
                (((1,), (1,)), ((), ())),
                preferred_element_type=f32,
            )
            total = product if total is None else total + product
    step = pl.program_id(0)
    rows, pairs = total.shape
    words = words_ref[...]
    words = jnp.broadcast_to(words[:, None, :], (words.shape[0], WORD_BITS, pairs))
    words = words.reshape(rows, pairs)
    row = lax.broadcasted_iota(jnp.int32, total.shape, 0)
    place = step * rows + row
    bit = lax.shift_right_logical(words, row & (WORD_BITS - 1)) & 1
    allowed = ((bit == 1) | (places[0] + place == 0)) & (place < count)
    masked = jnp.where(allowed, total, SENTINEL)
    out_ref[...] = masked

    @pl.when(step == 0)
    def _():
        top_ref[...] = jnp.full_like(top_ref, SENTINEL)
        sum_ref[...] = jnp.zeros_like(sum_ref)

    before = top_ref[...]
    top = jnp.maximum(before, jnp.max(masked, 0, keepdims=True))
    summed = sum_ref[...] * jnp.exp(before - top) + jnp.sum(
        jnp.where(allowed, jnp.exp(masked - top), 0.0), 0, keepdims=True
    )
    top_ref[...] = top
    sum_ref[...] = summed

    @pl.when(step == pl.num_programs(0) - 1)
    def _():
        share_ref[...] = jnp.where(
            summed > 0.0, top + jnp.log(jnp.maximum(summed, 1e-30)), SENTINEL
        )


def vocab_logits(places, w_rows, near, far, near_later, far_later, grammar_rows):
    count, depth = w_rows.shape
    pairs = PARTS * near[0].shape[1]
    blocks = [*near, far, *near_later, *far_later]

    def whole(block):
        return pl.BlockSpec(
            block.shape, lambda i, s: (0,) * block.ndim, pipeline_mode=pl.Buffered(1)
        )

    part = pl.BlockSpec((VOCAB_ROWS, pairs), lambda i, s: (i, 0))
    return pl.pallas_call(
        functools.partial(vocab_kernel, count),
        out_shape=(
            jax.ShapeDtypeStruct((count, pairs), f32),
            jax.ShapeDtypeStruct((1, pairs), f32),
        ),
        grid_spec=pltpu.PrefetchScalarGridSpec(
            num_scalar_prefetch=1,
            grid=(pl.cdiv(count, VOCAB_ROWS),),
            in_specs=[
                pl.BlockSpec((VOCAB_ROWS, depth), lambda i, s: (i, 0)),
                *(whole(block) for block in blocks),
                pl.BlockSpec((VOCAB_ROWS // WORD_BITS, pairs), lambda i, s: (i, 0)),
            ],
            out_specs=(part, pl.BlockSpec((1, pairs), lambda i, s: (0, 0))),
            scratch_shapes=[pltpu.VMEM((1, pairs), f32), pltpu.VMEM((1, pairs), f32)],
        ),
        compiler_params=pltpu.CompilerParams(vmem_limit_bytes=48 * 2**20),
        cost_estimate=pl.CostEstimate(
            flops=2 * count * pairs * depth, bytes_accessed=2 * count * depth, transcendentals=0
        ),
    )(places, w_rows, *blocks, grammar_rows)


def local(
    hidden_in,
    gain_attn,
    w_query,
    w_keyval,
    w_out,
    key_cache,
    value_cache,
    lengths,
    gain_final,
    w_vocab,
    pair_rows,
    grammar,
):
    local_rows = lengths.shape[0]
    row_count, features = hidden_in.shape
    query_cols = w_query.shape[1]
    group_count = w_keyval.shape[2] // HD
    x, z, c, y = (lax.axis_index(axis) for axis in ALL)
    pair_count = row_count // 2

    hidden_blocks = hidden_in.reshape(NX * NZ, NC, local_rows, features)
    gain_row = gain_attn.reshape(1, features)
    width = query_cols + w_keyval.shape[1] * w_keyval.shape[2]
    mine = project(1 - c, hidden_blocks, gain_row, w_query, w_keyval, None, 56)
    mine = project(c, hidden_blocks, gain_row, w_query, w_keyval, shift(mine, "c", 1), 24)
    mine = lax.all_to_all(mine.reshape(NX * NZ, local_rows, -1), ("x", "z"), 0, 0)
    mine = jnp.sum(mine.astype(f32), 0)
    projected = mine * lax.rsqrt(row_total(mine, width) / D + EPSILON)

    halves = HD // 2
    frequency = ROPE_BASE ** (-2.0 * jnp.arange(halves, dtype=f32) / HD)
    angles = lengths.astype(f32)[:, None] * frequency[None, :]
    cosine = jnp.cos(angles)[:, None, :]
    sin_part = jnp.sin(angles)[:, None, :]
    queries = rotate(
        projected[:, :query_cols].reshape(local_rows, query_cols // HD, HD), cosine, sin_part
    ).astype(bf16)
    kv_pairs = projected[:, query_cols:width].reshape(local_rows, 2, group_count, HD)
    new_key = rotate(kv_pairs[:, 0], cosine, sin_part).astype(bf16)
    new_value = kv_pairs[:, 1].astype(bf16)
    attended = attend(queries, new_key, new_value, key_cache, value_cache, lengths)

    share = local_rows // NY
    blocks = repeat(attended.reshape(NY, share, query_cols), NX * NZ)
    near = lax.all_to_all(blocks.reshape(-1, share, query_cols), ("x", "z", "y"), 0, 0)
    near, weights = lax.optimization_barrier((near, load(w_out, attended, 48 * 2**20)))
    near = near.reshape(NX * NZ, NY, share, query_cols).transpose(0, 2, 1, 3)
    near = near.reshape(NX * NZ * share, D)
    far = shift(near, "c", 1)
    near = jnp.dot(near, weights, preferred_element_type=f32)
    far = jnp.dot(far, weights, preferred_element_type=f32)
    update = jnp.concatenate([jnp.where(c == 0, near, far), jnp.where(c == 0, far, near)], 0)

    hidden_here = lax.dynamic_index_in_dim(
        hidden_in.reshape(NX * NZ, NC, NY, share, features), y, 2, False
    )
    hidden_here = hidden_here.transpose(1, 0, 2, 3).reshape(-1, features)
    residual = (hidden_here.astype(f32) + update).astype(bf16)
    rounded = residual.astype(f32)
    held = residual.shape[0]
    scaled = (rounded * gain_final).astype(bf16)
    got = {by: shift(scaled, "y", by) for by in SHIFTS}
    quarters = jnp.arange(NY, dtype=jnp.int32)

    def rows_of(order):
        row = (
            jnp.arange(NX * NZ, dtype=jnp.int32)[None, None, :, None] * NC
            + jnp.arange(NC, dtype=jnp.int32)[None, :, None, None]
        ) * local_rows
        row = row + order[:, None, None, None] * share
        return (row + jnp.arange(share, dtype=jnp.int32)).reshape(-1)

    grid = pair_rows.reshape(PARTS, pair_count // PARTS, 2).transpose(0, 2, 1).reshape(-1, 1)
    pick = (grid == rows_of((y - quarters + NY) % NY)[None, :]).astype(bf16)
    order = jnp.arange(row_count, dtype=jnp.int32)
    place = jnp.sum(jnp.where(grid == rows_of(quarters)[None, :], order[None, :], 0), 1)

    parts = pick_rows(pick, [scaled, got[1], got[2], got[3]])
    squares_out = jnp.sum(rounded * rounded, 1)
    shares = lax.all_to_all(
        jnp.broadcast_to(squares_out, (NX * NZ * NC * NY, SQUARES_COPIES, held)), ALL, 0, 0
    )[:, 0]
    parts = join([(part, swap(part, i, 0)) for i, part in enumerate(parts)], False)
    parts = [(part, swap(part, i, 1)) for i, part in enumerate(parts)]
    shares, first = lax.optimization_barrier((shares, parts[0][1]))
    parts[0] = (parts[0][0], first)
    parts = guide_pairs(shares, place[:, None], parts)
    *near, together = join([(part, swap(part, i, 2)) for i, part in enumerate(parts)], True)
    far = shift(together, "c", 1)
    near_later = [swap(part, i, 3) for i, part in enumerate(near)]
    far_later = [shift(part, "c", 1) for part in near_later]

    columns = []
    for core in range(NC):
        for distance in range(NX * NZ):
            where = {"x": x, "z": z}
            for bit, (axis, by) in enumerate(SWAPS):
                if distance >> bit & 1:
                    where[axis] = where[axis] ^ by
            columns.append(((where["x"] * NZ + where["z"]) * NC + (c + core) % NC) * features)
    offset = lax.axis_index(ALL) * w_vocab.shape[1]
    guided = vocab_logits(
        jnp.stack([offset, *columns]).astype(jnp.int32),
        w_vocab.T,
        near,
        far,
        near_later,
        far_later,
        grammar.T,
    )
    masked, shares = guided
    shares = lax.all_to_all(
        jnp.broadcast_to(shares[0], (NX * NZ * NC * NY, pair_count)), ALL, 0, 0
    )
    highest = jnp.max(shares, 0)
    total = highest + jnp.log(jnp.sum(jnp.exp(shares - highest), 0))
    return jnp.where(masked > 0.5 * SENTINEL, masked - total[None, :], 0.0).T


def solution(mesh):
    split = Mesh(mesh.devices.reshape(NX, NZ, NC, NY), ALL)
    in_specs = (
        P(None, DP),
        P(DP),
        P(DP, "y"),
        P(DP, None, "y"),
        P(None, DP),
        P(DP, "y", None, None),
        P(DP, "y", None, None),
        P(DP),
        P(DP),
        P(None, ALL),
        P(),
        P(None, ALL),
    )
    out_specs = P(None, ALL)
    return jax.shard_map(local, mesh=split, in_specs=in_specs, out_specs=out_specs, check_vma=False)
```

```python
import functools

import jax
import jax.numpy as jnp
from jax import lax
from jax.experimental import pallas as pl
from jax.experimental.pallas import tpu as pltpu
from jax.sharding import Mesh
from jax.sharding import PartitionSpec as P

D = 8192
HD = 128
NX, NZ, NC, NY = 4, 4, 2, 4
DP = ("x", "z", "c")
ALL = ("x", "z", "c", "y")

GUIDANCE = 3.0
ROPE_BASE = 500000.0
EPSILON = 1e-05
SENTINEL = -1e30
VOCAB_ROWS = 256
WORD_BITS = 16
SHIFTS = (1, 3, 2)
SWAPS = (("x", 1), ("x", 3), ("z", 1), ("z", 3))
PARTS = 4
ORDERS = ((0, 1, 2, 3), (0, 1, 3, 2), (2, 3, 0, 1), (2, 3, 1, 0))
GROUPS = 2
SQUARES_COPIES = 4
bf16 = jnp.bfloat16
f32 = jnp.float32


def shift(value, axis, by):
    size = lax.axis_size(axis)
    return lax.ppermute(value, axis, [(i, (i + by) % size) for i in range(size)])


def swap(value, part, step):
    axis, by = SWAPS[ORDERS[part][step]]
    return lax.ppermute(value, axis, [(i, i ^ by) for i in range(lax.axis_size(axis))])


def slot_of(part, distance):
    return sum((distance >> bit & 1) << step for step, bit in enumerate(ORDERS[part]))


def rotate(values, cosine, sin_part):
    halves = values.shape[-1] // 2
    leading = values[..., :halves]
    trailing = values[..., halves:]
    return jnp.concatenate(
        [leading * cosine - trailing * sin_part, trailing * cosine + leading * sin_part], -1
    )


def attend(queries, new_key, new_value, key_cache, value_cache, lengths):
    rows, groups = (key_cache.shape[0], key_cache.shape[1])
    group_size = queries.shape[1] // groups
    scaling = queries.shape[2] ** (-0.5)
    grouped = queries.reshape(rows, groups, group_size, -1)
    scores = (
        jnp.einsum("rgqd,rgld->rgql", grouped, key_cache, preferred_element_type=f32)
        * scaling
    )
    fresh = (
        jnp.einsum("rgqd,rgd->rgq", grouped, new_key, preferred_element_type=f32) * scaling
    )
    usable = jnp.arange(key_cache.shape[2], dtype=jnp.int32)[None, :] < lengths[:, None]
    scores = jnp.where(usable[:, None, None, :], scores, SENTINEL)
    highest = jnp.maximum(jnp.max(scores, -1), fresh)
    weights = jnp.where(usable[:, None, None, :], jnp.exp(scores - highest[..., None]), 0.0)
    fresh_weight = jnp.exp(fresh - highest)
    summed = jnp.sum(weights, -1) + fresh_weight
    probs_cache = (weights / summed[..., None]).astype(bf16)
    probs_fresh = (fresh_weight / summed).astype(bf16)
    mixed = jnp.einsum(
        "rgql,rgld->rgqd", probs_cache, value_cache, preferred_element_type=f32
    )
    mixed = (
        mixed
        + probs_fresh.astype(f32)[..., None] * new_value.astype(f32)[:, :, None, :]
    )
    return mixed.reshape(rows, -1).astype(bf16)


def row_total(values, width):
    return values[..., width : width + 1] + values[..., width + 1 : width + 2]


def small_cost(flops, moved):
    return pl.CostEstimate(flops=flops, bytes_accessed=moved, transcendentals=0)


def load_kernel(w_ref, after_ref, out_ref, arrived):
    copy = pltpu.make_async_copy(w_ref, out_ref, arrived)
    copy.start()
    copy.wait()


def load(weights, after, limit):
    hbm = pl.BlockSpec(memory_space=pl.ANY)
    return pl.pallas_call(
        load_kernel,
        out_shape=pltpu.VMEM(weights.shape, weights.dtype),
        in_specs=[hbm, hbm],
        out_specs=pl.BlockSpec(memory_space=pltpu.VMEM),
        scratch_shapes=[pltpu.SemaphoreType.DMA],
        compiler_params=pltpu.CompilerParams(vmem_limit_bytes=limit),
        cost_estimate=pl.CostEstimate(
            flops=0, bytes_accessed=2 * weights.size * weights.dtype.itemsize, transcendentals=0
        ),
    )(weights, after)


def repeat_kernel(block_ref, out_ref):
    for copy in range(out_ref.shape[0]):
        out_ref[copy] = block_ref[...]


def repeat(block, copies):
    whole = pl.BlockSpec(memory_space=pltpu.VMEM)
    return pl.pallas_call(
        repeat_kernel,
        out_shape=jax.ShapeDtypeStruct((copies,) + block.shape, block.dtype),
        in_specs=[whole],
        out_specs=whole,
        compiler_params=pltpu.CompilerParams(vmem_limit_bytes=12 * 2**20),
        cost_estimate=small_cost(0, 2 * (copies + 1) * block.size),
    )(block)


def project_kernel(core_ref, hidden_ref, gain_ref, query_ref, keyval_ref, *refs):
    got_ref = refs[0] if len(refs) == 2 else None
    out_ref = refs[-1]
    blocks, _, local_rows, features = hidden_ref.shape
    rows = blocks * local_rows
    values = hidden_ref[:, core_ref[0]].reshape(rows, features).astype(f32)
    total = jnp.sum(values * values, 1, keepdims=True)
    gained = (values * gain_ref[...]).astype(bf16)
    query_cols = query_ref.shape[1]
    key_cols = keyval_ref.shape[2]
    width = query_cols + 2 * key_cols
    extra = out_ref.shape[1] - width

    def put(part, sums):
        if got_ref is not None:
            sums = sums + got_ref[:, part].astype(f32)
        out_ref[:, part] = sums.astype(bf16)

    put(slice(0, query_cols), jnp.dot(gained, query_ref[...], preferred_element_type=f32))
    for half in range(2):
        start = query_cols + half * key_cols
        sums = jnp.dot(gained, keyval_ref[:, half, :], preferred_element_type=f32)
        put(slice(start, start + key_cols), sums)
    if got_ref is not None:
        parts = got_ref[:, width:].astype(f32)
        total = total + parts[:, 0:1] + parts[:, 1:2]
    high = total.astype(bf16).astype(f32)
    column = lax.broadcasted_iota(jnp.int32, (rows, extra), 1)
    squares = jnp.where(column == 0, high, jnp.where(column == 1, total - high, 0.0))
    out_ref[:, width:] = squares.astype(bf16)


def project(core, hidden, gain, w_query, w_keyval, got, limit):
    blocks, _, local_rows, features = hidden.shape
    rows = blocks * local_rows
    width = w_query.shape[1] + w_keyval.shape[1] * w_keyval.shape[2] + 128
    operands = [hidden, gain, w_query, w_keyval] + ([] if got is None else [got])
    whole = pl.BlockSpec(memory_space=pltpu.VMEM)
    return pl.pallas_call(
        project_kernel,
        out_shape=jax.ShapeDtypeStruct((rows, width), bf16),
        in_specs=[pl.BlockSpec(memory_space=pltpu.SMEM)] + [whole] * len(operands),
        out_specs=whole,
        compiler_params=pltpu.CompilerParams(vmem_limit_bytes=limit * 2**20),
        cost_estimate=pl.CostEstimate(
            flops=2 * rows * width * features, bytes_accessed=4 * rows * width, transcendentals=0
        ),
    )(core.reshape(1).astype(jnp.int32), *operands)


def pick_kernel(pick_ref, *refs):
    blocks, outs = refs[:NY], refs[NY:]
    held = blocks[0].shape[0]
    rows = outs[0].shape[1]
    for part, out_ref in enumerate(outs):
        lines = slice(part * rows, (part + 1) * rows)
        total = None
        for quarter, block in enumerate(blocks):
            chosen = pick_ref[lines, quarter * held : (quarter + 1) * held]
            product = jnp.dot(chosen, block[...], preferred_element_type=f32)
            total = product if total is None else total + product
        out_ref[0] = total.astype(bf16)


def pick_rows(pick, blocks):
    whole = pl.BlockSpec(memory_space=pltpu.VMEM)
    shape = (1, pick.shape[0] // GROUPS, blocks[0].shape[1])
    return pl.pallas_call(
        pick_kernel,
        out_shape=[jax.ShapeDtypeStruct(shape, bf16)] * GROUPS,
        in_specs=[whole] * (1 + len(blocks)),
        out_specs=[whole] * GROUPS,
        compiler_params=pltpu.CompilerParams(vmem_limit_bytes=12 * 2**20),
        cost_estimate=small_cost(2 * pick.size * blocks[0].shape[1], pick.size * 4),
    )(pick, *blocks)


def join_kernel(*refs):
    parts = len(refs) // 3
    ins, outs = refs[: 2 * parts], refs[2 * parts :]
    count = ins[0].shape[0]
    for part in range(parts):
        for half in range(2):
            value = ins[2 * part + half][...]
            lines = slice(half * count, (half + 1) * count)
            outs[part][lines] = value
            if len(outs) > parts:
                outs[parts][part, lines] = value


def join(pairs, together):
    whole = pl.BlockSpec(memory_space=pltpu.VMEM)
    count, *rest = pairs[0][0].shape
    parts = len(pairs)
    shapes = [jax.ShapeDtypeStruct((2 * count, *rest), bf16)] * parts
    if together:
        shapes.append(jax.ShapeDtypeStruct((parts, 2 * count, *rest), bf16))
    return pl.pallas_call(
        join_kernel,
        out_shape=shapes,
        in_specs=[whole] * (2 * parts),
        out_specs=[whole] * len(shapes),
        compiler_params=pltpu.CompilerParams(vmem_limit_bytes=12 * 2**20),
        cost_estimate=small_cost(0, 16 * PARTS * pairs[0][0].size),
    )(*(half for pair in pairs for half in pair))


def guide_kernel(shares_ref, place_ref, *refs):
    ins, outs = refs[: 2 * GROUPS], refs[2 * GROUPS :]
    devices, held = shares_ref.shape
    total = jnp.sum(shares_ref[...].reshape(devices // NY, NY, held), 0)
    scale = lax.rsqrt(total / D + EPSILON)
    place = place_ref[...]
    lane = lax.broadcasted_iota(jnp.int32, (place.shape[0], held), 1)
    chosen = jnp.zeros((place.shape[0], held), f32)
    for quarter in range(NY):
        here = lane + quarter * held == place
        chosen = chosen + jnp.where(here, scale[quarter : quarter + 1, :], 0.0)
    chosen = jnp.sum(chosen, 1, keepdims=True)
    parts_each = PARTS // GROUPS
    rows = ins[0].shape[1] // parts_each
    half = rows // 2
    for part in range(PARTS):
        kept = GUIDANCE * chosen[part * rows : part * rows + half]
        taken = (GUIDANCE - 1.0) * chosen[part * rows + half : (part + 1) * rows]
        first = part % parts_each * rows
        for slot in range(outs[part].shape[0]):
            ref = ins[part // parts_each * 2 + slot // 2]
            both = kept * ref[slot % 2, first : first + half, :].astype(f32)
            both = both - taken * ref[slot % 2, first + half : first + rows, :].astype(f32)
            outs[part][slot] = both.astype(bf16)


def guide_pairs(shares, place, pairs):
    _, rows, features = pairs[0][0].shape
    whole = pl.BlockSpec(memory_space=pltpu.VMEM)
    return pl.pallas_call(
        guide_kernel,
        out_shape=[jax.ShapeDtypeStruct((4, rows * GROUPS // PARTS // 2, features), bf16)] * PARTS,
        in_specs=[whole] * (2 + 2 * GROUPS),
        out_specs=[whole] * PARTS,
        compiler_params=pltpu.CompilerParams(vmem_limit_bytes=12 * 2**20),
        cost_estimate=small_cost(0, 16 * PARTS * pairs[0][0].size),
    )(shares, place, *(half for pair in pairs for half in pair))


def vocab_kernel(count, places, w_ref, *refs):
    near, far, near_later, far_later = (
        refs[:PARTS],
        refs[PARTS],
        refs[PARTS + 1 : 2 * PARTS + 1],
        refs[2 * PARTS + 1 : 3 * PARTS + 1],
    )
    words_ref, out_ref, share_ref, top_ref, sum_ref = refs[3 * PARTS + 1 :]
    features = near[0].shape[2]
    early = near[0].shape[0]

    def piece(core, part, slot):
        if slot >= early:
            return (far_later if core else near_later)[part][slot - early]
        return far[part, slot] if core else near[part][slot]

    total = None
    for core in range(NC):
        for distance in range(NX * NZ):
            start = pl.multiple_of(places[1 + core * NX * NZ + distance], features)
            held = [piece(core, part, slot_of(part, distance)) for part in range(PARTS)]
            product = lax.dot_general(
                w_ref[:, pl.ds(start, features)],
                jnp.concatenate(held, 0),
                (((1,), (1,)), ((), ())),
                preferred_element_type=f32,
            )
            total = product if total is None else total + product
    step = pl.program_id(0)
    rows, pairs = total.shape
    words = words_ref[...]
    words = jnp.broadcast_to(words[:, None, :], (words.shape[0], WORD_BITS, pairs))
    words = words.reshape(rows, pairs)
    row = lax.broadcasted_iota(jnp.int32, total.shape, 0)
    place = step * rows + row
    bit = lax.shift_right_logical(words, row & (WORD_BITS - 1)) & 1
    allowed = ((bit == 1) | (places[0] + place == 0)) & (place < count)
    masked = jnp.where(allowed, total, SENTINEL)
    out_ref[...] = masked

    @pl.when(step == 0)
    def _():
        top_ref[...] = jnp.full_like(top_ref, SENTINEL)
        sum_ref[...] = jnp.zeros_like(sum_ref)

    before = top_ref[...]
    top = jnp.maximum(before, jnp.max(masked, 0, keepdims=True))
    summed = sum_ref[...] * jnp.exp(before - top) + jnp.sum(
        jnp.where(allowed, jnp.exp(masked - top), 0.0), 0, keepdims=True
    )
    top_ref[...] = top
    sum_ref[...] = summed

    @pl.when(step == pl.num_programs(0) - 1)
    def _():
        share_ref[...] = jnp.where(
            summed > 0.0, top + jnp.log(jnp.maximum(summed, 1e-30)), SENTINEL
        )


def vocab_logits(places, w_rows, near, far, near_later, far_later, grammar_rows):
    count, depth = w_rows.shape
    pairs = PARTS * near[0].shape[1]
    blocks = [*near, far, *near_later, *far_later]

    def whole(block):
        return pl.BlockSpec(
            block.shape, lambda i, s: (0,) * block.ndim, pipeline_mode=pl.Buffered(1)
        )

    part = pl.BlockSpec((VOCAB_ROWS, pairs), lambda i, s: (i, 0))
    return pl.pallas_call(
        functools.partial(vocab_kernel, count),
        out_shape=(
            jax.ShapeDtypeStruct((count, pairs), f32),
            jax.ShapeDtypeStruct((1, pairs), f32),
        ),
        grid_spec=pltpu.PrefetchScalarGridSpec(
            num_scalar_prefetch=1,
            grid=(pl.cdiv(count, VOCAB_ROWS),),
            in_specs=[
                pl.BlockSpec((VOCAB_ROWS, depth), lambda i, s: (i, 0)),
                *(whole(block) for block in blocks),
                pl.BlockSpec((VOCAB_ROWS // WORD_BITS, pairs), lambda i, s: (i, 0)),
            ],
            out_specs=(part, pl.BlockSpec((1, pairs), lambda i, s: (0, 0))),
            scratch_shapes=[pltpu.VMEM((1, pairs), f32), pltpu.VMEM((1, pairs), f32)],
        ),
        compiler_params=pltpu.CompilerParams(vmem_limit_bytes=48 * 2**20),
        cost_estimate=pl.CostEstimate(
            flops=2 * count * pairs * depth, bytes_accessed=2 * count * depth, transcendentals=0
        ),
    )(places, w_rows, *blocks, grammar_rows)


def local(
    hidden_in,
    gain_attn,
    w_query,
    w_keyval,
    w_out,
    key_cache,
    value_cache,
    lengths,
    gain_final,
    w_vocab,
    pair_rows,
    grammar,
):
    local_rows = lengths.shape[0]
    row_count, features = hidden_in.shape
    query_cols = w_query.shape[1]
    group_count = w_keyval.shape[2] // HD
    x, z, c, y = (lax.axis_index(axis) for axis in ALL)
    pair_count = row_count // 2

    hidden_blocks = hidden_in.reshape(NX * NZ, NC, local_rows, features)
    gain_row = gain_attn.reshape(1, features)
    width = query_cols + w_keyval.shape[1] * w_keyval.shape[2]
    mine = project(1 - c, hidden_blocks, gain_row, w_query, w_keyval, None, 56)
    mine = project(c, hidden_blocks, gain_row, w_query, w_keyval, shift(mine, "c", 1), 24)
    mine = lax.all_to_all(mine.reshape(NX * NZ, local_rows, -1), ("x", "z"), 0, 0)
    mine = jnp.sum(mine.astype(f32), 0)
    projected = mine * lax.rsqrt(row_total(mine, width) / D + EPSILON)

    halves = HD // 2
    frequency = ROPE_BASE ** (-2.0 * jnp.arange(halves, dtype=f32) / HD)
    angles = lengths.astype(f32)[:, None] * frequency[None, :]
    cosine = jnp.cos(angles)[:, None, :]
    sin_part = jnp.sin(angles)[:, None, :]
    queries = rotate(
        projected[:, :query_cols].reshape(local_rows, query_cols // HD, HD), cosine, sin_part
    ).astype(bf16)
    kv_pairs = projected[:, query_cols:width].reshape(local_rows, 2, group_count, HD)
    new_key = rotate(kv_pairs[:, 0], cosine, sin_part).astype(bf16)
    new_value = kv_pairs[:, 1].astype(bf16)
    attended = attend(queries, new_key, new_value, key_cache, value_cache, lengths)

    share = local_rows // NY
    blocks = repeat(attended.reshape(NY, share, query_cols), NX * NZ)
    near = lax.all_to_all(blocks.reshape(-1, share, query_cols), ("x", "z", "y"), 0, 0)
    near, weights = lax.optimization_barrier((near, load(w_out, attended, 48 * 2**20)))
    near = near.reshape(NX * NZ, NY, share, query_cols).transpose(0, 2, 1, 3)
    near = near.reshape(NX * NZ * share, D)
    far = shift(near, "c", 1)
    near = jnp.dot(near, weights, preferred_element_type=f32)
    far = jnp.dot(far, weights, preferred_element_type=f32)
    update = jnp.concatenate([jnp.where(c == 0, near, far), jnp.where(c == 0, far, near)], 0)

    hidden_here = lax.dynamic_index_in_dim(
        hidden_in.reshape(NX * NZ, NC, NY, share, features), y, 2, False
    )
    hidden_here = hidden_here.transpose(1, 0, 2, 3).reshape(-1, features)
    residual = (hidden_here.astype(f32) + update).astype(bf16)
    rounded = residual.astype(f32)
    held = residual.shape[0]
    scaled = (rounded * gain_final).astype(bf16)
    got = {by: shift(scaled, "y", by) for by in SHIFTS}
    quarters = jnp.arange(NY, dtype=jnp.int32)

    def rows_of(order):
        row = (
            jnp.arange(NX * NZ, dtype=jnp.int32)[None, None, :, None] * NC
            + jnp.arange(NC, dtype=jnp.int32)[None, :, None, None]
        ) * local_rows
        row = row + order[:, None, None, None] * share
        return (row + jnp.arange(share, dtype=jnp.int32)).reshape(-1)

    grid = pair_rows.reshape(PARTS, pair_count // PARTS, 2).transpose(0, 2, 1).reshape(-1, 1)
    pick = (grid == rows_of((y - quarters + NY) % NY)[None, :]).astype(bf16)
    order = jnp.arange(row_count, dtype=jnp.int32)
    place = jnp.sum(jnp.where(grid == rows_of(quarters)[None, :], order[None, :], 0), 1)

    groups = pick_rows(pick, [scaled, got[1], got[2], got[3]])
    squares_out = jnp.sum(rounded * rounded, 1)
    shares = lax.all_to_all(
        jnp.broadcast_to(squares_out, (NX * NZ * NC * NY, SQUARES_COPIES, held)), ALL, 0, 0
    )[:, 0]
    first_parts = range(0, PARTS, PARTS // GROUPS)
    groups = join([(group, swap(group, i, 0)) for i, group in zip(first_parts, groups)], False)
    groups = [(group, swap(group, i, 1)) for i, group in zip(first_parts, groups)]
    shares, first = lax.optimization_barrier((shares, groups[0][1]))
    groups[0] = (groups[0][0], first)
    parts = guide_pairs(shares, place[:, None], groups)
    *near, together = join([(part, swap(part, i, 2)) for i, part in enumerate(parts)], True)
    far = shift(together, "c", 1)
    near_later = [swap(part, i, 3) for i, part in enumerate(near)]
    far_later = [shift(part, "c", 1) for part in near_later]

    columns = []
    for core in range(NC):
        for distance in range(NX * NZ):
            where = {"x": x, "z": z}
            for bit, (axis, by) in enumerate(SWAPS):
                if distance >> bit & 1:
                    where[axis] = where[axis] ^ by
            columns.append(((where["x"] * NZ + where["z"]) * NC + (c + core) % NC) * features)
    offset = lax.axis_index(ALL) * w_vocab.shape[1]
    guided = vocab_logits(
        jnp.stack([offset, *columns]).astype(jnp.int32),
        w_vocab.T,
        near,
        far,
        near_later,
        far_later,
        grammar.T,
    )
    masked, shares = guided
    shares = lax.all_to_all(
        jnp.broadcast_to(shares[0], (NX * NZ * NC * NY, pair_count)), ALL, 0, 0
    )
    highest = jnp.max(shares, 0)
    total = highest + jnp.log(jnp.sum(jnp.exp(shares - highest), 0))
    return jnp.where(masked > 0.5 * SENTINEL, masked - total[None, :], 0.0).T


def solution(mesh):
    split = Mesh(mesh.devices.reshape(NX, NZ, NC, NY), ALL)
    in_specs = (
        P(None, DP),
        P(DP),
        P(DP, "y"),
        P(DP, None, "y"),
        P(None, DP),
        P(DP, "y", None, None),
        P(DP, "y", None, None),
        P(DP),
        P(DP),
        P(None, ALL),
        P(),
        P(None, ALL),
    )
    out_specs = P(None, ALL)
    return jax.shard_map(local, mesh=split, in_specs=in_specs, out_specs=out_specs, check_vma=False)
```

```python
import functools

import jax
import jax.numpy as jnp
from jax import lax
from jax.experimental import pallas as pl
from jax.experimental.pallas import tpu as pltpu
from jax.sharding import Mesh
from jax.sharding import PartitionSpec as P

D = 8192
HD = 128
NX, NZ, NC, NY = 4, 4, 2, 4
DP = ("x", "z", "c")
ALL = ("x", "z", "c", "y")

GUIDANCE = 3.0
ROPE_BASE = 500000.0
EPSILON = 1e-05
SENTINEL = -1e30
VOCAB_ROWS = 256
WORD_BITS = 16
SHIFTS = (1, 3, 2)
SWAPS = (("x", 1), ("x", 3), ("z", 1), ("z", 3))
PARTS = 4
ORDERS = ((0, 1, 2, 3), (0, 1, 3, 2), (2, 3, 0, 1), (2, 3, 1, 0))
GROUPS = 2
SQUARES_COPIES = 8
bf16 = jnp.bfloat16
f32 = jnp.float32


def shift(value, axis, by):
    size = lax.axis_size(axis)
    return lax.ppermute(value, axis, [(i, (i + by) % size) for i in range(size)])


def swap(value, part, step):
    axis, by = SWAPS[ORDERS[part][step]]
    return lax.ppermute(value, axis, [(i, i ^ by) for i in range(lax.axis_size(axis))])


def slot_of(part, distance):
    return sum((distance >> bit & 1) << step for step, bit in enumerate(ORDERS[part]))


def rotate(values, cosine, sin_part):
    halves = values.shape[-1] // 2
    leading = values[..., :halves]
    trailing = values[..., halves:]
    return jnp.concatenate(
        [leading * cosine - trailing * sin_part, trailing * cosine + leading * sin_part], -1
    )


def attend(queries, new_key, new_value, key_cache, value_cache, lengths):
    rows, groups = (key_cache.shape[0], key_cache.shape[1])
    group_size = queries.shape[1] // groups
    scaling = queries.shape[2] ** (-0.5)
    grouped = queries.reshape(rows, groups, group_size, -1)
    scores = (
        jnp.einsum("rgqd,rgld->rgql", grouped, key_cache, preferred_element_type=f32)
        * scaling
    )
    fresh = (
        jnp.einsum("rgqd,rgd->rgq", grouped, new_key, preferred_element_type=f32) * scaling
    )
    usable = jnp.arange(key_cache.shape[2], dtype=jnp.int32)[None, :] < lengths[:, None]
    scores = jnp.where(usable[:, None, None, :], scores, SENTINEL)
    highest = jnp.maximum(jnp.max(scores, -1), fresh)
    weights = jnp.where(usable[:, None, None, :], jnp.exp(scores - highest[..., None]), 0.0)
    fresh_weight = jnp.exp(fresh - highest)
    summed = jnp.sum(weights, -1) + fresh_weight
    probs_cache = (weights / summed[..., None]).astype(bf16)
    probs_fresh = (fresh_weight / summed).astype(bf16)
    mixed = jnp.einsum(
        "rgql,rgld->rgqd", probs_cache, value_cache, preferred_element_type=f32
    )
    mixed = (
        mixed
        + probs_fresh.astype(f32)[..., None] * new_value.astype(f32)[:, :, None, :]
    )
    return mixed.reshape(rows, -1).astype(bf16)


def row_total(values, width):
    return values[..., width : width + 1] + values[..., width + 1 : width + 2]


def small_cost(flops, moved):
    return pl.CostEstimate(flops=flops, bytes_accessed=moved, transcendentals=0)


def load_kernel(w_ref, after_ref, out_ref, arrived):
    copy = pltpu.make_async_copy(w_ref, out_ref, arrived)
    copy.start()
    copy.wait()


def load(weights, after, limit):
    hbm = pl.BlockSpec(memory_space=pl.ANY)
    return pl.pallas_call(
        load_kernel,
        out_shape=pltpu.VMEM(weights.shape, weights.dtype),
        in_specs=[hbm, hbm],
        out_specs=pl.BlockSpec(memory_space=pltpu.VMEM),
        scratch_shapes=[pltpu.SemaphoreType.DMA],
        compiler_params=pltpu.CompilerParams(vmem_limit_bytes=limit),
        cost_estimate=pl.CostEstimate(
            flops=0, bytes_accessed=2 * weights.size * weights.dtype.itemsize, transcendentals=0
        ),
    )(weights, after)


def repeat_kernel(block_ref, out_ref):
    for copy in range(out_ref.shape[0]):
        out_ref[copy] = block_ref[...]


def repeat(block, copies):
    whole = pl.BlockSpec(memory_space=pltpu.VMEM)
    return pl.pallas_call(
        repeat_kernel,
        out_shape=jax.ShapeDtypeStruct((copies,) + block.shape, block.dtype),
        in_specs=[whole],
        out_specs=whole,
        compiler_params=pltpu.CompilerParams(vmem_limit_bytes=12 * 2**20),
        cost_estimate=small_cost(0, 2 * (copies + 1) * block.size),
    )(block)


def project_kernel(core_ref, hidden_ref, gain_ref, query_ref, keyval_ref, *refs):
    got_ref = refs[0] if len(refs) == 2 else None
    out_ref = refs[-1]
    blocks, _, local_rows, features = hidden_ref.shape
    rows = blocks * local_rows
    values = hidden_ref[:, core_ref[0]].reshape(rows, features).astype(f32)
    total = jnp.sum(values * values, 1, keepdims=True)
    gained = (values * gain_ref[...]).astype(bf16)
    query_cols = query_ref.shape[1]
    key_cols = keyval_ref.shape[2]
    width = query_cols + 2 * key_cols
    extra = out_ref.shape[1] - width

    def put(part, sums):
        if got_ref is not None:
            sums = sums + got_ref[:, part].astype(f32)
        out_ref[:, part] = sums.astype(bf16)

    put(slice(0, query_cols), jnp.dot(gained, query_ref[...], preferred_element_type=f32))
    for half in range(2):
        start = query_cols + half * key_cols
        sums = jnp.dot(gained, keyval_ref[:, half, :], preferred_element_type=f32)
        put(slice(start, start + key_cols), sums)
    if got_ref is not None:
        parts = got_ref[:, width:].astype(f32)
        total = total + parts[:, 0:1] + parts[:, 1:2]
    high = total.astype(bf16).astype(f32)
    column = lax.broadcasted_iota(jnp.int32, (rows, extra), 1)
    squares = jnp.where(column == 0, high, jnp.where(column == 1, total - high, 0.0))
    out_ref[:, width:] = squares.astype(bf16)


def project(core, hidden, gain, w_query, w_keyval, got, limit):
    blocks, _, local_rows, features = hidden.shape
    rows = blocks * local_rows
    width = w_query.shape[1] + w_keyval.shape[1] * w_keyval.shape[2] + 128
    operands = [hidden, gain, w_query, w_keyval] + ([] if got is None else [got])
    whole = pl.BlockSpec(memory_space=pltpu.VMEM)
    return pl.pallas_call(
        project_kernel,
        out_shape=jax.ShapeDtypeStruct((rows, width), bf16),
        in_specs=[pl.BlockSpec(memory_space=pltpu.SMEM)] + [whole] * len(operands),
        out_specs=whole,
        compiler_params=pltpu.CompilerParams(vmem_limit_bytes=limit * 2**20),
        cost_estimate=pl.CostEstimate(
            flops=2 * rows * width * features, bytes_accessed=4 * rows * width, transcendentals=0
        ),
    )(core.reshape(1).astype(jnp.int32), *operands)


def pick_kernel(pick_ref, *refs):
    blocks, outs = refs[:NY], refs[NY:]
    held = blocks[0].shape[0]
    rows = outs[0].shape[1]
    for part, out_ref in enumerate(outs):
        lines = slice(part * rows, (part + 1) * rows)
        total = None
        for quarter, block in enumerate(blocks):
            chosen = pick_ref[lines, quarter * held : (quarter + 1) * held]
            product = jnp.dot(chosen, block[...], preferred_element_type=f32)
            total = product if total is None else total + product
        out_ref[0] = total.astype(bf16)


def pick_rows(pick, blocks):
    whole = pl.BlockSpec(memory_space=pltpu.VMEM)
    shape = (1, pick.shape[0] // GROUPS, blocks[0].shape[1])
    return pl.pallas_call(
        pick_kernel,
        out_shape=[jax.ShapeDtypeStruct(shape, bf16)] * GROUPS,
        in_specs=[whole] * (1 + len(blocks)),
        out_specs=[whole] * GROUPS,
        compiler_params=pltpu.CompilerParams(vmem_limit_bytes=12 * 2**20),
        cost_estimate=small_cost(2 * pick.size * blocks[0].shape[1], pick.size * 4),
    )(pick, *blocks)


def join_kernel(*refs):
    parts = len(refs) // 3
    ins, outs = refs[: 2 * parts], refs[2 * parts :]
    count = ins[0].shape[0]
    for part in range(parts):
        for half in range(2):
            value = ins[2 * part + half][...]
            lines = slice(half * count, (half + 1) * count)
            outs[part][lines] = value
            if len(outs) > parts:
                outs[parts][part, lines] = value


def join(pairs, together):
    whole = pl.BlockSpec(memory_space=pltpu.VMEM)
    count, *rest = pairs[0][0].shape
    parts = len(pairs)
    shapes = [jax.ShapeDtypeStruct((2 * count, *rest), bf16)] * parts
    if together:
        shapes.append(jax.ShapeDtypeStruct((parts, 2 * count, *rest), bf16))
    return pl.pallas_call(
        join_kernel,
        out_shape=shapes,
        in_specs=[whole] * (2 * parts),
        out_specs=[whole] * len(shapes),
        compiler_params=pltpu.CompilerParams(vmem_limit_bytes=12 * 2**20),
        cost_estimate=small_cost(0, 16 * PARTS * pairs[0][0].size),
    )(*(half for pair in pairs for half in pair))


def guide_kernel(shares_ref, place_ref, *refs):
    ins, outs = refs[: 2 * GROUPS], refs[2 * GROUPS :]
    devices, held = shares_ref.shape
    total = jnp.sum(shares_ref[...].reshape(devices // NY, NY, held), 0)
    scale = lax.rsqrt(total / D + EPSILON)
    place = place_ref[...]
    lane = lax.broadcasted_iota(jnp.int32, (place.shape[0], held), 1)
    chosen = jnp.zeros((place.shape[0], held), f32)
    for quarter in range(NY):
        here = lane + quarter * held == place
        chosen = chosen + jnp.where(here, scale[quarter : quarter + 1, :], 0.0)
    chosen = jnp.sum(chosen, 1, keepdims=True)
    parts_each = PARTS // GROUPS
    rows = ins[0].shape[1] // parts_each
    half = rows // 2
    for part in range(PARTS):
        kept = GUIDANCE * chosen[part * rows : part * rows + half]
        taken = (GUIDANCE - 1.0) * chosen[part * rows + half : (part + 1) * rows]
        first = part % parts_each * rows
        for slot in range(outs[part].shape[0]):
            ref = ins[part // parts_each * 2 + slot // 2]
            both = kept * ref[slot % 2, first : first + half, :].astype(f32)
            both = both - taken * ref[slot % 2, first + half : first + rows, :].astype(f32)
            outs[part][slot] = both.astype(bf16)


def guide_pairs(shares, place, pairs):
    _, rows, features = pairs[0][0].shape
    whole = pl.BlockSpec(memory_space=pltpu.VMEM)
    return pl.pallas_call(
        guide_kernel,
        out_shape=[jax.ShapeDtypeStruct((4, rows * GROUPS // PARTS // 2, features), bf16)] * PARTS,
        in_specs=[whole] * (2 + 2 * GROUPS),
        out_specs=[whole] * PARTS,
        compiler_params=pltpu.CompilerParams(vmem_limit_bytes=12 * 2**20),
        cost_estimate=small_cost(0, 16 * PARTS * pairs[0][0].size),
    )(shares, place, *(half for pair in pairs for half in pair))


def vocab_kernel(count, places, w_ref, *refs):
    near, far, near_later, far_later = (
        refs[:PARTS],
        refs[PARTS],
        refs[PARTS + 1 : 2 * PARTS + 1],
        refs[2 * PARTS + 1 : 3 * PARTS + 1],
    )
    words_ref, out_ref, share_ref, top_ref, sum_ref = refs[3 * PARTS + 1 :]
    features = near[0].shape[2]
    early = near[0].shape[0]

    def piece(core, part, slot):
        if slot >= early:
            return (far_later if core else near_later)[part][slot - early]
        return far[part, slot] if core else near[part][slot]

    total = None
    for core in range(NC):
        for distance in range(NX * NZ):
            start = pl.multiple_of(places[1 + core * NX * NZ + distance], features)
            held = [piece(core, part, slot_of(part, distance)) for part in range(PARTS)]
            product = lax.dot_general(
                w_ref[:, pl.ds(start, features)],
                jnp.concatenate(held, 0),
                (((1,), (1,)), ((), ())),
                preferred_element_type=f32,
            )
            total = product if total is None else total + product
    step = pl.program_id(0)
    rows, pairs = total.shape
    words = words_ref[...]
    words = jnp.broadcast_to(words[:, None, :], (words.shape[0], WORD_BITS, pairs))
    words = words.reshape(rows, pairs)
    row = lax.broadcasted_iota(jnp.int32, total.shape, 0)
    place = step * rows + row
    bit = lax.shift_right_logical(words, row & (WORD_BITS - 1)) & 1
    allowed = ((bit == 1) | (places[0] + place == 0)) & (place < count)
    masked = jnp.where(allowed, total, SENTINEL)
    out_ref[...] = masked

    @pl.when(step == 0)
    def _():
        top_ref[...] = jnp.full_like(top_ref, SENTINEL)
        sum_ref[...] = jnp.zeros_like(sum_ref)

    before = top_ref[...]
    top = jnp.maximum(before, jnp.max(masked, 0, keepdims=True))
    summed = sum_ref[...] * jnp.exp(before - top) + jnp.sum(
        jnp.where(allowed, jnp.exp(masked - top), 0.0), 0, keepdims=True
    )
    top_ref[...] = top
    sum_ref[...] = summed

    @pl.when(step == pl.num_programs(0) - 1)
    def _():
        share_ref[...] = jnp.where(
            summed > 0.0, top + jnp.log(jnp.maximum(summed, 1e-30)), SENTINEL
        )


def vocab_logits(places, w_rows, near, far, near_later, far_later, grammar_rows):
    count, depth = w_rows.shape
    pairs = PARTS * near[0].shape[1]
    blocks = [*near, far, *near_later, *far_later]

    def whole(block):
        return pl.BlockSpec(
            block.shape, lambda i, s: (0,) * block.ndim, pipeline_mode=pl.Buffered(1)
        )

    part = pl.BlockSpec((VOCAB_ROWS, pairs), lambda i, s: (i, 0))
    return pl.pallas_call(
        functools.partial(vocab_kernel, count),
        out_shape=(
            jax.ShapeDtypeStruct((count, pairs), f32),
            jax.ShapeDtypeStruct((1, pairs), f32),
        ),
        grid_spec=pltpu.PrefetchScalarGridSpec(
            num_scalar_prefetch=1,
            grid=(pl.cdiv(count, VOCAB_ROWS),),
            in_specs=[
                pl.BlockSpec((VOCAB_ROWS, depth), lambda i, s: (i, 0)),
                *(whole(block) for block in blocks),
                pl.BlockSpec((VOCAB_ROWS // WORD_BITS, pairs), lambda i, s: (i, 0)),
            ],
            out_specs=(part, pl.BlockSpec((1, pairs), lambda i, s: (0, 0))),
            scratch_shapes=[pltpu.VMEM((1, pairs), f32), pltpu.VMEM((1, pairs), f32)],
        ),
        compiler_params=pltpu.CompilerParams(vmem_limit_bytes=48 * 2**20),
        cost_estimate=pl.CostEstimate(
            flops=2 * count * pairs * depth, bytes_accessed=2 * count * depth, transcendentals=0
        ),
    )(places, w_rows, *blocks, grammar_rows)


def local(
    hidden_in,
    gain_attn,
    w_query,
    w_keyval,
    w_out,
    key_cache,
    value_cache,
    lengths,
    gain_final,
    w_vocab,
    pair_rows,
    grammar,
):
    local_rows = lengths.shape[0]
    row_count, features = hidden_in.shape
    query_cols = w_query.shape[1]
    group_count = w_keyval.shape[2] // HD
    x, z, c, y = (lax.axis_index(axis) for axis in ALL)
    pair_count = row_count // 2

    hidden_blocks = hidden_in.reshape(NX * NZ, NC, local_rows, features)
    gain_row = gain_attn.reshape(1, features)
    width = query_cols + w_keyval.shape[1] * w_keyval.shape[2]
    mine = project(1 - c, hidden_blocks, gain_row, w_query, w_keyval, None, 56)
    mine = project(c, hidden_blocks, gain_row, w_query, w_keyval, shift(mine, "c", 1), 24)
    mine = lax.all_to_all(mine.reshape(NX * NZ, local_rows, -1), ("x", "z"), 0, 0)
    mine = jnp.sum(mine.astype(f32), 0)
    projected = mine * lax.rsqrt(row_total(mine, width) / D + EPSILON)

    halves = HD // 2
    frequency = ROPE_BASE ** (-2.0 * jnp.arange(halves, dtype=f32) / HD)
    angles = lengths.astype(f32)[:, None] * frequency[None, :]
    cosine = jnp.cos(angles)[:, None, :]
    sin_part = jnp.sin(angles)[:, None, :]
    queries = rotate(
        projected[:, :query_cols].reshape(local_rows, query_cols // HD, HD), cosine, sin_part
    ).astype(bf16)
    kv_pairs = projected[:, query_cols:width].reshape(local_rows, 2, group_count, HD)
    new_key = rotate(kv_pairs[:, 0], cosine, sin_part).astype(bf16)
    new_value = kv_pairs[:, 1].astype(bf16)
    attended = attend(queries, new_key, new_value, key_cache, value_cache, lengths)

    share = local_rows // NY
    blocks = repeat(attended.reshape(NY, share, query_cols), NX * NZ)
    near = lax.all_to_all(blocks.reshape(-1, share, query_cols), ("x", "z", "y"), 0, 0)
    near, weights = lax.optimization_barrier((near, load(w_out, attended, 48 * 2**20)))
    near = near.reshape(NX * NZ, NY, share, query_cols).transpose(0, 2, 1, 3)
    near = near.reshape(NX * NZ * share, D)
    far = shift(near, "c", 1)
    near = jnp.dot(near, weights, preferred_element_type=f32)
    far = jnp.dot(far, weights, preferred_element_type=f32)
    update = jnp.concatenate([jnp.where(c == 0, near, far), jnp.where(c == 0, far, near)], 0)

    hidden_here = lax.dynamic_index_in_dim(
        hidden_in.reshape(NX * NZ, NC, NY, share, features), y, 2, False
    )
    hidden_here = hidden_here.transpose(1, 0, 2, 3).reshape(-1, features)
    residual = (hidden_here.astype(f32) + update).astype(bf16)
    rounded = residual.astype(f32)
    held = residual.shape[0]
    scaled = (rounded * gain_final).astype(bf16)
    got = {by: shift(scaled, "y", by) for by in SHIFTS}
    quarters = jnp.arange(NY, dtype=jnp.int32)

    def rows_of(order):
        row = (
            jnp.arange(NX * NZ, dtype=jnp.int32)[None, None, :, None] * NC
            + jnp.arange(NC, dtype=jnp.int32)[None, :, None, None]
        ) * local_rows
        row = row + order[:, None, None, None] * share
        return (row + jnp.arange(share, dtype=jnp.int32)).reshape(-1)

    grid = pair_rows.reshape(PARTS, pair_count // PARTS, 2).transpose(0, 2, 1).reshape(-1, 1)
    pick = (grid == rows_of((y - quarters + NY) % NY)[None, :]).astype(bf16)
    order = jnp.arange(row_count, dtype=jnp.int32)
    place = jnp.sum(jnp.where(grid == rows_of(quarters)[None, :], order[None, :], 0), 1)

    groups = pick_rows(pick, [scaled, got[1], got[2], got[3]])
    squares_out = jnp.sum(rounded * rounded, 1)
    shares = lax.all_to_all(
        jnp.broadcast_to(squares_out, (NX * NZ * NC * NY, SQUARES_COPIES, held)), ALL, 0, 0
    )[:, 0]
    first_parts = range(0, PARTS, PARTS // GROUPS)
    groups = join([(group, swap(group, i, 0)) for i, group in zip(first_parts, groups)], False)
    groups = [(group, swap(group, i, 1)) for i, group in zip(first_parts, groups)]
    shares, first = lax.optimization_barrier((shares, groups[0][1]))
    groups[0] = (groups[0][0], first)
    parts = guide_pairs(shares, place[:, None], groups)
    *near, together = join([(part, swap(part, i, 2)) for i, part in enumerate(parts)], True)
    far = shift(together, "c", 1)
    near_later = [swap(part, i, 3) for i, part in enumerate(near)]
    far_later = [shift(part, "c", 1) for part in near_later]

    columns = []
    for core in range(NC):
        for distance in range(NX * NZ):
            where = {"x": x, "z": z}
            for bit, (axis, by) in enumerate(SWAPS):
                if distance >> bit & 1:
                    where[axis] = where[axis] ^ by
            columns.append(((where["x"] * NZ + where["z"]) * NC + (c + core) % NC) * features)
    offset = lax.axis_index(ALL) * w_vocab.shape[1]
    guided = vocab_logits(
        jnp.stack([offset, *columns]).astype(jnp.int32),
        w_vocab.T,
        near,
        far,
        near_later,
        far_later,
        grammar.T,
    )
    masked, shares = guided
    shares = lax.all_to_all(
        jnp.broadcast_to(shares[0], (NX * NZ * NC * NY, pair_count)), ALL, 0, 0
    )
    highest = jnp.max(shares, 0)
    total = highest + jnp.log(jnp.sum(jnp.exp(shares - highest), 0))
    return jnp.where(masked > 0.5 * SENTINEL, masked - total[None, :], 0.0).T


def solution(mesh):
    split = Mesh(mesh.devices.reshape(NX, NZ, NC, NY), ALL)
    in_specs = (
        P(None, DP),
        P(DP),
        P(DP, "y"),
        P(DP, None, "y"),
        P(None, DP),
        P(DP, "y", None, None),
        P(DP, "y", None, None),
        P(DP),
        P(DP),
        P(None, ALL),
        P(),
        P(None, ALL),
    )
    out_specs = P(None, ALL)
    return jax.shard_map(local, mesh=split, in_specs=in_specs, out_specs=out_specs, check_vma=False)
```
